128 devices in a mesh: row: 16 (over z_lo, y, core), col: 8 (over z_hi, x).
Axes of the slice: x: 4, y: 4, z: 4 (z_hi: 2, z_lo: 2; z = z_hi * 2 + z_lo), core: 2. Of those that a mesh axis runs over, the one named last changes fastest.
Arguments:
- image: bfloat16 [512, 1024, 256], P('row', 'col'), may hold values from -60 to 60
- bn_gain: float32 [256], replicated, may hold values from 0.5 to 2
- bn_shift: float32 [256], replicated, may hold values from -3 to 3
- expand_weight: bfloat16 [256, 1024], replicated, may hold values from -0.375 to 0.375
- expand_bias: float32 [1024], replicated, may hold values from -3 to 3
- depth_kernel: bfloat16 [3, 3, 1024], replicated, may hold values from -2 to 2
- depth_bias: float32 [1024], replicated, may hold values from -3 to 3
- project_weight: bfloat16 [1024, 256], replicated, may hold values from -0.1875 to 0.1875
- norm_gain: float32 [2, 256], replicated, may hold values from 0.5 to 2
- qkv_weight: bfloat16 [2, 256, 768], replicated, may hold values from -7 to 7
- out_weight: bfloat16 [2, 256, 256], replicated, may hold values from -0.375 to 0.375
Outputs:
- features_out: bfloat16 [512, 1024, 256], P('row', 'col')
The draws below stay inside these ranges and needn't reach their ends.
All inputs are finite; a program needn't handle non-finite values.
Results may differ from the reference program's by a relative error of at most 0.011.
Values may be sent and summed in bfloat16 or wider, within the bound.
No kernel may reach another device: no remote copies, remote signals or barrier semaphores. Data moves between devices by JAX's collectives and lax.ppermute only.
A program may use at most 128 MiB of HBM per device.

```python
import math
import jax
import jax.numpy as jnp
from jax import lax

CHANNELS = 256
HEADS = 8
HIDDEN_CH = 1024
WINDOW = 8
GRID_SIDE = 16
GRID_ROWS = 512
GRID_COLS = 1024


def draw_image(key, part):
    key = jax.random.fold_in(key, 11)
    keys = jax.random.split(key, 1)
    field = jnp.clip(jax.random.normal(keys[0], (GRID_ROWS, GRID_COLS, CHANNELS), jnp.float32), -6.0, 6.0)
    return field.astype(jnp.bfloat16)


def draw_qkv_weight(key, part):
    key = jax.random.fold_in(key, 23)
    keys = jax.random.split(key, 1)
    base = jnp.clip(jax.random.normal(keys[0], (2, CHANNELS, 3 * CHANNELS), jnp.float32), -5.0, 5.0) / math.sqrt(CHANNELS)
    return base.astype(jnp.bfloat16)


def gaussian(key, shape, width, bound, dtype=jnp.bfloat16):
    return jnp.clip(width * jax.random.normal(key, shape, jnp.float32), -bound, bound).astype(dtype)


def setup_inputs(seed: int = 0) -> dict:
    key_of = jax.random.split(jax.random.key(seed), 12)
    image = draw_image(jax.random.fold_in(key_of[11], 71), 0)
    bn_gain = jnp.clip(jnp.exp(jax.random.uniform(key_of[1], (CHANNELS,), jnp.float32, math.log(0.5), math.log(2.0))), 0.5, 2.0)
    bn_shift = gaussian(key_of[2], (CHANNELS,), 0.5, 3.0, jnp.float32)
    expand_weight = gaussian(key_of[3], (CHANNELS, HIDDEN_CH), CHANNELS ** -0.5, 0.375)
    expand_bias = gaussian(key_of[4], (HIDDEN_CH,), 0.5, 3.0, jnp.float32)
    depth_kernel = gaussian(key_of[5], (3, 3, HIDDEN_CH), 9 ** -0.5, 2.0)
    depth_bias = gaussian(key_of[6], (HIDDEN_CH,), 0.5, 3.0, jnp.float32)
    project_weight = gaussian(key_of[7], (HIDDEN_CH, CHANNELS), HIDDEN_CH ** -0.5, 0.1875)
    norm_gain = jnp.clip(jnp.exp(jax.random.uniform(key_of[8], (2, CHANNELS), jnp.float32, math.log(0.5), math.log(2.0))), 0.5, 2.0)
    qkv_weight = draw_qkv_weight(jax.random.fold_in(key_of[11], 71), 0)
    out_weight = gaussian(key_of[10], (2, CHANNELS, CHANNELS), CHANNELS ** -0.5, 0.375)
    return dict(image=image, bn_gain=bn_gain, bn_shift=bn_shift, expand_weight=expand_weight, expand_bias=expand_bias, depth_kernel=depth_kernel, depth_bias=depth_bias, project_weight=project_weight, norm_gain=norm_gain, qkv_weight=qkv_weight, out_weight=out_weight)


def layer_norm(values, gain):
    mean = lax.optimization_barrier(jnp.mean(values, axis=-1, keepdims=True))
    centred = values - mean
    spread = lax.optimization_barrier(jnp.mean(centred * centred, axis=-1, keepdims=True))
    return centred * lax.rsqrt(spread + 1e-05) * gain

def attend(tokens, gain, qkv_weight, out_weight):
    groups, length, chans = tokens.shape
    values = tokens.astype(jnp.float32)
    normed = layer_norm(values, gain).astype(jnp.bfloat16)
    proj = jnp.dot(normed.reshape(groups * length, chans), qkv_weight, preferred_element_type=jnp.float32).astype(jnp.bfloat16)
    proj = proj.reshape(groups, length, 3, HEADS, chans // HEADS)
    query = proj[:, :, 0].astype(jnp.float32)
    keys = proj[:, :, 1].astype(jnp.float32)
    vals = proj[:, :, 2].astype(jnp.float32)
    scores = jnp.einsum('gqhd,gkhd->ghqk', query, keys) * (chans // HEADS) ** (-0.5)
    top = lax.optimization_barrier(jnp.max(scores, axis=-1, keepdims=True))
    weights = jnp.exp(scores - top)
    probs = (weights / lax.optimization_barrier(jnp.sum(weights, axis=-1, keepdims=True))).astype(jnp.bfloat16)
    mixed = jnp.einsum('ghqk,gkhd->gqhd', probs.astype(jnp.float32), vals).astype(jnp.bfloat16)
    moved = jnp.dot(mixed.reshape(groups * length, chans), out_weight, preferred_element_type=jnp.float32)
    return (values + moved.reshape(groups, length, chans)).astype(jnp.bfloat16)

def reference(image, bn_gain, bn_shift, expand_weight, expand_bias, depth_kernel, depth_bias, project_weight, norm_gain, qkv_weight, out_weight):
    rows, cols, chans = image.shape
    wide = expand_weight.shape[1]
    strip = 16
    padded = jnp.pad(image, ((1, 1), (0, 0), (0, 0)))
    kernel = depth_kernel.astype(jnp.float32)

    def one_strip(index):
        start = index.astype(jnp.int32) * strip
        piece = lax.dynamic_slice_in_dim(padded, start, strip + 2, 0)
        normed = (piece.astype(jnp.float32) * bn_gain + bn_shift).astype(jnp.bfloat16)
        hidden = jnp.dot(normed.reshape(-1, chans), expand_weight, preferred_element_type=jnp.float32) + expand_bias
        hidden = jax.nn.gelu(hidden).astype(jnp.bfloat16).reshape(strip + 2, cols, wide)
        row_ids = start - 1 + jnp.arange(strip + 2).astype(jnp.int32)
        keep = (row_ids >= 0) & (row_ids < rows)
        hidden = jnp.where(keep[:, None, None], hidden, jnp.zeros_like(hidden))
        hidden = jnp.pad(hidden, ((0, 0), (1, 1), (0, 0)))
        total = jnp.zeros((strip, cols, wide), jnp.float32)
        for down in range(3):
            for across in range(3):
                total = total + hidden[down:down + strip, across:across + cols].astype(jnp.float32) * kernel[down, across]
        middle = jax.nn.gelu(total + depth_bias).astype(jnp.bfloat16)
        moved = jnp.dot(middle.reshape(-1, wide), project_weight, preferred_element_type=jnp.float32)
        return (piece[1:strip + 1].astype(jnp.float32) + moved.reshape(strip, cols, chans)).astype(jnp.bfloat16)
    after_conv = lax.map(one_strip, jnp.arange(rows // strip)).reshape(rows, cols, chans)
    wins = after_conv.reshape(rows // WINDOW, WINDOW, cols // WINDOW, WINDOW, chans).transpose(0, 2, 1, 3, 4)
    wins = wins.reshape(rows // WINDOW, cols // WINDOW, WINDOW * WINDOW, chans)

    def block_row(group):
        return attend(group, norm_gain[0], qkv_weight[0], out_weight[0])
    done = lax.map(block_row, wins)
    after_block = done.reshape(rows // WINDOW, cols // WINDOW, WINDOW, WINDOW, chans).transpose(0, 2, 1, 3, 4).reshape(rows, cols, chans)
    stride_row = rows // GRID_SIDE
    stride_col = cols // GRID_SIDE
    sets = after_block.reshape(GRID_SIDE, stride_row, GRID_SIDE, stride_col, chans).transpose(1, 3, 0, 2, 4)
    sets = sets.reshape(stride_row, stride_col, GRID_SIDE * GRID_SIDE, chans)

    def grid_row(group):
        return attend(group, norm_gain[1], qkv_weight[1], out_weight[1])
    finished = lax.map(grid_row, sets)
    finished = finished.reshape(stride_row, stride_col, GRID_SIDE, GRID_SIDE, chans).transpose(2, 0, 3, 1, 4)
    return finished.reshape(rows, cols, chans)
```

```python
import jax
import jax.numpy as jnp
from jax import lax
from jax.experimental import pallas as pl
from jax.experimental.pallas import tpu as pltpu
from jax.sharding import PartitionSpec as P

HEADS = 8
HEAD = 32
CH = 256
HID = 1024
WINDOW = 8
EPS = 1e-5
GELU_A = 0.7978845608028654
GELU_B = 0.7978845608028654 * 0.044715
QSCALE = 32.0**-0.5 * 1.4426950408889634
BF = jnp.bfloat16
F32 = jnp.float32


def mm(a, b, dims):
    return lax.dot_general(a, b, (dims, ((), ())), preferred_element_type=F32)


def nn(a, b):
    return mm(a, b, ((1,), (0,)))


def nt(a, b):
    return mm(a, b, ((1,), (1,)))


def tn(a, b):
    return mm(a, b, ((0,), (0,)))


def twice_gelu(x):
    inner = x * (x * x * jnp.asarray(GELU_B, x.dtype) + jnp.asarray(GELU_A, x.dtype))
    return x + x * jnp.tanh(inner)


def normalised(y, gain):
    mean = jnp.mean(y, axis=-1, keepdims=True)
    centred = y - mean
    spread = jnp.mean(centred * centred, axis=-1, keepdims=True)
    return centred * lax.rsqrt(spread + EPS) * gain


def store_halves(ref, at, values):
    ref[0, at, :] = values[:, :128]
    ref[1, at, :] = values[:, 128:]


def load_halves(ref, at):
    return jnp.concatenate([ref[0, at, :], ref[1, at, :]], axis=1)


def qkv_of(xn, wk, wqv):
    keys = nn(xn, wk).astype(BF)
    turned = nt(wqv, xn)
    return (turned[:CH] * QSCALE).astype(BF), keys, turned[CH:].astype(BF)


def window_mix(xn, wk, wqv):
    query, keys, vals = qkv_of(xn, wk, wqv)
    lane = lax.broadcasted_iota(jnp.int32, (HEAD, 128), 1)
    first = lane < 64
    first_keys = lax.broadcasted_iota(jnp.int32, (64, 128), 1) < 64
    none = jnp.zeros((HEAD, 128), BF)
    ones = jnp.ones((16, 128), BF)
    pairs = []
    for p in range(2):
        rows = []
        for g in range(2):
            lhs = jnp.concatenate(
                [
                    keys[128 * p : 128 * p + 64, 128 * g : 128 * g + 128],
                    keys[128 * p + 64 : 128 * p + 128, 128 * g : 128 * g + 128],
                ],
                axis=1,
            )
            cols = []
            for j in range(4):
                h = 4 * g + j
                q = query[HEAD * h : HEAD * h + HEAD, 128 * p : 128 * p + 128]
                parts = [none] * 8
                parts[j] = jnp.where(first, q, none)
                parts[4 + j] = jnp.where(first, none, q)
                cols.append(jnp.concatenate(parts, axis=0))
            scores = nn(lhs, jnp.concatenate(cols, axis=1))
            top = jnp.max(scores, axis=0, keepdims=True)
            probs = jnp.exp2((scores - top).astype(BF))
            for j in range(0, 4, 2):
                h = 4 * g + j
                blocks = []
                for i in range(2):
                    ph = probs[:, 128 * (j + i) : 128 * (j + i) + 128]
                    zero = jnp.zeros_like(ph)
                    blocks.append(
                        jnp.concatenate(
                            [jnp.where(first_keys, ph, zero), jnp.where(first_keys, zero, ph)], axis=0
                        )
                    )
                left = jnp.concatenate(
                    [vals[HEAD * h : HEAD * h + 2 * HEAD, 128 * p : 128 * p + 128], ones], axis=0
                )
                out = nn(left, jnp.concatenate(blocks, axis=1))
                inv = 1.0 / out[64:65]
                rows.append((out[:32, :128] * inv[:, :128]).astype(BF))
                rows.append((out[32:64, 128:] * inv[:, 128:]).astype(BF))
        pairs.append(jnp.concatenate(rows, axis=0))
    return jnp.concatenate(pairs, axis=1)


def grid_mix(xn, wk, wqv):
    query, keys, vals = qkv_of(xn, wk, wqv)
    none = jnp.zeros((HEAD, 256), BF)
    ones = jnp.ones((16, 256), BF)
    rows = []
    for h in range(HEADS):
        g, j = divmod(h, 4)
        parts = [none] * 4
        parts[j] = query[HEAD * h : HEAD * h + HEAD]
        scores = nn(keys[:, 128 * g : 128 * g + 128], jnp.concatenate(parts, axis=0))
        top = jnp.max(scores, axis=0, keepdims=True)
        probs = jnp.exp2((scores - top).astype(BF))
        out = nn(jnp.concatenate([vals[HEAD * h : HEAD * h + HEAD], ones], axis=0), probs)
        rows.append((out[:HEAD] * (1.0 / out[HEAD : HEAD + 1])).astype(BF))
    return jnp.concatenate(rows, axis=0)


def front_kernel(
    edge_ref,
    image_ref,
    above_ref,
    below_ref,
    sides_ref,
    bn_gain_ref,
    bn_shift_ref,
    expand_ref,
    expand_bias_ref,
    depth_ref,
    depth_bias_ref,
    project_ref,
    gain_ref,
    wk_ref,
    wqv_ref,
    wo_ref,
    out_ref,
    line,
    hidden,
    side_hidden,
    middle,
    moved,
):
    step = pl.program_id(0)
    strips = pl.num_programs(0)
    rows_dev = image_ref.shape[0]
    cell = lax.broadcasted_iota(jnp.int32, (16, 1), 0)

    def normed(values):
        return values.astype(F32) * bn_gain_ref[...] + bn_shift_ref[...]

    def activated(cells, c):
        lanes = slice(256 * c, 256 * c + 256)
        total = nn(cells, expand_ref[:, lanes]) + expand_bias_ref[:, lanes]
        return twice_gelu(total.astype(BF))

    def expand_row(values, row, keep):
        store_halves(line, slice(None), normed(values))
        cells = jnp.concatenate(
            [load_halves(line, pl.ds(m, 16, stride=WINDOW)) for m in range(WINDOW)], axis=0
        ).astype(BF)
        for c in range(HID // 256):
            lanes = slice(256 * c, 256 * c + 256)
            act = activated(cells, c)
            if keep is not None:
                act = act * keep
            act = act.reshape(WINDOW, 16, 256)
            hidden[row, 1 : WINDOW + 1, :, lanes] = act
            left = pltpu.roll(act[WINDOW - 1].astype(F32), 1, 0)
            right = pltpu.roll(act[0].astype(F32), 15, 0)
            left = jnp.where(cell == 0, side_hidden[pl.ds(row, 1), lanes], left)
            right = jnp.where(cell == 15, side_hidden[pl.ds(40 + row, 1), lanes], right)
            hidden[row, 0, :, lanes] = left.astype(BF)
            hidden[row, WINDOW + 1, :, lanes] = right.astype(BF)

    @pl.when(step == 0)
    def _():
        cells = normed(sides_ref[...]).astype(BF)
        index = lax.broadcasted_iota(jnp.int32, (80, 1), 0)
        right = index >= 40
        row = jnp.where(right, index - 40, index)
        keep = jnp.where(right, edge_ref[3], edge_ref[2])
        keep = jnp.where(row == 0, keep * edge_ref[0], keep)
        keep = jnp.where(row == rows_dev + 1, keep * edge_ref[1], keep)
        keep = keep.astype(F32)
        for c in range(HID // 256):
            lanes = slice(256 * c, 256 * c + 256)
            side_hidden[:, lanes] = activated(cells, c).astype(F32) * keep
        expand_row(above_ref[...], 0, edge_ref[0].astype(F32).astype(BF))
        expand_row(image_ref[0], 1, None)

    def expand_step(i, carry):
        expand_row(image_ref[step * WINDOW + 1 + i], step * WINDOW + 2 + i, None)
        return carry

    lax.fori_loop(0, jnp.where(step == strips - 1, WINDOW - 1, WINDOW), expand_step, 0)

    @pl.when(step == strips - 1)
    def _():
        expand_row(below_ref[...], rows_dev + 1, edge_ref[1].astype(F32).astype(BF))

    def depth_step(r, carry):
        for c in range(HID // 128):
            lanes = slice(128 * c, 128 * c + 128)
            total = None
            for down in range(3):
                around = hidden[step * WINDOW + r + down, :, :, lanes]
                for across in range(3):
                    term = around[across : across + WINDOW] * depth_ref[3 * down + across, :, lanes]
                    total = term if total is None else total + term
            act = twice_gelu(total + depth_bias_ref[:, lanes])
            middle[pl.ds(pl.multiple_of(r * 128, 128), 128), lanes] = act.reshape(128, 128)
        return carry

    lax.fori_loop(0, WINDOW, depth_step, 0)

    for part in range(4):
        at = slice(256 * part, 256 * part + 256)
        store_halves(moved, at, nn(middle[at, :], project_ref[...]))

    def quad_step(i, carry):
        pieces = []
        for p in range(2):
            col = pl.multiple_of(32 * i + 16 * p, 16)
            res = image_ref[pl.ds(step * WINDOW, WINDOW), pl.ds(col, 16), :].astype(F32)
            res = res.reshape(WINDOW, 2, WINDOW, CH)
            for w in range(2):
                conv = load_halves(moved, pl.ds(4 * i + 2 * p + w, 64, stride=16))
                pieces.append(res[:, w].reshape(64, CH) + conv)
        y = jnp.concatenate(pieces, axis=0)
        xn = normalised(y, gain_ref[...]).astype(BF)
        mixed = window_mix(xn, wk_ref[...], wqv_ref[...])
        y = (y + tn(mixed, wo_ref[...])).astype(BF)
        out_ref[0, pl.ds(4 * lax.rem(i, 2), 4), :, lax.div(i, 2)] = y.reshape(4, 4, 16, CH)
        return carry

    lax.fori_loop(0, 4, quad_step, 0)


def grid_kernel(tokens_ref, gain_ref, wk_ref, wqv_ref, wo_ref, out_ref, work):
    def norm_step(i, carry):
        at = pl.ds(pl.multiple_of(16 * i, 16), 16)
        y = tokens_ref[at].astype(F32).reshape(256, CH)
        rows = pl.ds(pl.multiple_of(256 * i, 256), 256)
        store_halves(work, rows, normalised(y, gain_ref[...]))
        return carry

    lax.fori_loop(0, 16, norm_step, 0)

    def set_step(k, carry):
        at = pl.ds(k, 256, stride=16)
        xn = load_halves(work, at).astype(BF)
        mixed = grid_mix(xn, wk_ref[...], wqv_ref[...])
        store_halves(work, at, tn(mixed, wo_ref[...]))
        return carry

    lax.fori_loop(0, 16, set_step, 0)

    def add_step(i, carry):
        at = pl.ds(pl.multiple_of(16 * i, 16), 16)
        y = load_halves(work, pl.ds(pl.multiple_of(256 * i, 256), 256)).reshape(16, 16, CH)
        out_ref[at] = (tokens_ref[at].astype(F32) + y).astype(BF)
        return carry

    lax.fori_loop(0, 16, add_step, 0)


def whole(shape):
    return pl.BlockSpec(shape, lambda i: (0,) * len(shape))


def front(edge, image, above, below, sides, params):
    rows_dev, cols_dev, chans = image.shape
    strips = rows_dev // WINDOW
    args = (image, above, below, sides) + params
    return pl.pallas_call(
        front_kernel,
        grid=(strips,),
        in_specs=[pl.BlockSpec(memory_space=pltpu.SMEM)] + [whole(a.shape) for a in args],
        out_specs=pl.BlockSpec((1, 8, 4, 2, 16, chans), lambda i: (i, 0, 0, 0, 0, 0)),
        out_shape=jax.ShapeDtypeStruct((strips, 8, 4, 2, 16, chans), BF),
        scratch_shapes=[
            pltpu.VMEM((2, cols_dev, 128), F32),
            pltpu.VMEM((rows_dev + 2, WINDOW + 2, 16, HID), BF),
            pltpu.VMEM((80, HID), F32),
            pltpu.VMEM((WINDOW * cols_dev, HID), BF),
            pltpu.VMEM((2, WINDOW * cols_dev, 128), F32),
        ],
        compiler_params=pltpu.CompilerParams(
            dimension_semantics=("arbitrary",), vmem_limit_bytes=48 * 2**20
        ),
        name="front",
    )(edge, *args)


def grid_attention(tokens, gain, wk, wqv, wo):
    args = (tokens, gain, wk, wqv, wo)
    return pl.pallas_call(
        grid_kernel,
        grid=(1,),
        in_specs=[whole(a.shape) for a in args],
        out_specs=whole(tokens.shape),
        out_shape=jax.ShapeDtypeStruct(tokens.shape, BF),
        scratch_shapes=[pltpu.VMEM((2, tokens.shape[0] * tokens.shape[1], 128), F32)],
        compiler_params=pltpu.CompilerParams(
            dimension_semantics=("arbitrary",), vmem_limit_bytes=40 * 2**20
        ),
        name="grid_attention",
    )(*args)


def halos(image):
    rows = lax.axis_size("row")
    cols = lax.axis_size("col")
    up = [(i, i + 1) for i in range(rows - 1)]
    down = [(i + 1, i) for i in range(rows - 1)]
    above = lax.ppermute(image[-1:], "row", up)
    below = lax.ppermute(image[:1], "row", down)
    first = jnp.concatenate([above[:, :1], image[:, :1], below[:, :1]], axis=0)[:, 0]
    last = jnp.concatenate([above[:, -1:], image[:, -1:], below[:, -1:]], axis=0)[:, 0]
    left = lax.ppermute(last, "col", [(i, i + 1) for i in range(cols - 1)])
    right = lax.ppermute(first, "col", [(i + 1, i) for i in range(cols - 1)])
    pad = ((0, 40 - left.shape[0]), (0, 0))
    sides = jnp.concatenate([jnp.pad(left, pad), jnp.pad(right, pad)], axis=0)
    return above[0], below[0], sides


def split_qkv(weight):
    wq, wk, wv = weight[:, :CH], weight[:, CH : 2 * CH], weight[:, 2 * CH :]
    return wk, jnp.concatenate([wq, wv], axis=1).T


def per_device(
    image,
    bn_gain,
    bn_shift,
    expand_weight,
    expand_bias,
    depth_kernel,
    depth_bias,
    project_weight,
    norm_gain,
    qkv_weight,
    out_weight,
):
    rows_dev, cols_dev, chans = image.shape
    row_at = lax.axis_index("row")
    col_at = lax.axis_index("col")
    edge = jnp.stack(
        [
            row_at > 0,
            row_at < lax.axis_size("row") - 1,
            col_at > 0,
            col_at < lax.axis_size("col") - 1,
        ]
    ).astype(jnp.int32)
    above, below, sides = halos(image)
    wk0, wqv0 = split_qkv(qkv_weight[0])
    wk1, wqv1 = split_qkv(qkv_weight[1])
    depth = jnp.broadcast_to((depth_kernel * 0.5).astype(BF).reshape(9, 1, HID), (9, 16, HID))
    params = (
        bn_gain[None],
        bn_shift[None],
        expand_weight,
        expand_bias[None],
        depth,
        jnp.broadcast_to(depth_bias.astype(BF)[None], (16, HID)),
        project_weight * jnp.asarray(0.5, BF),
        norm_gain[:1],
        wk0,
        wqv0,
        out_weight[0],
    )
    after_block = front(edge, image, above, below, sides, params)
    outgoing = after_block.reshape(128, 32, chans)
    received = lax.all_to_all(outgoing, ("row", "col"), split_axis=0, concat_axis=0, tiled=True)
    done = grid_attention(received.reshape(256, 16, chans), norm_gain[1:], wk1, wqv1, out_weight[1])
    returned = lax.all_to_all(
        done.reshape(128, 32, chans), ("row", "col"), split_axis=0, concat_axis=0, tiled=True
    )
    placed = returned.reshape(4, 8, 4, 2, 2, 8, chans).transpose(0, 2, 4, 3, 1, 5, 6)
    return placed.reshape(rows_dev, cols_dev, chans)


def solution(mesh):
    in_specs = (P("row", "col", None), P(), P(), P(), P(), P(), P(), P(), P(), P(), P())
    out_specs = P("row", "col", None)
    return jax.shard_map(
        per_device, mesh=mesh, in_specs=in_specs, out_specs=out_specs, check_vma=False
    )
```

```python
import jax
import jax.numpy as jnp
from jax import lax
from jax.experimental import pallas as pl
from jax.experimental.pallas import tpu as pltpu
from jax.sharding import PartitionSpec as P

HEADS = 8
SETS = 4
AHEAD = 4
WAHEAD = 2


HEAD = 32
CH = 256
HID = 1024
WINDOW = 8
EPS = 1e-5
GELU_A = 0.7978845608028654
CUBE = (GELU_A * 0.044715) ** (1.0 / 3.0)
GELU_C = GELU_A / CUBE
QSCALE = 32.0**-0.5 * 1.4426950408889634
BF = jnp.bfloat16
F32 = jnp.float32


def mm(a, b, dims):
    return lax.dot_general(a, b, (dims, ((), ())), preferred_element_type=F32)


def nn(a, b):
    return mm(a, b, ((1,), (0,)))


def nt(a, b):
    return mm(a, b, ((1,), (1,)))


def tn(a, b):
    return mm(a, b, ((0,), (0,)))


def scaled_gelu(z):
    return z + z * jnp.tanh(z * (z * z + GELU_C))


def normalised(y, gain):
    mean = jnp.mean(y, axis=-1, keepdims=True)
    centred = y - mean
    spread = jnp.mean(centred * centred, axis=-1, keepdims=True)
    return centred * lax.rsqrt(spread + EPS) * gain


def run(parts):
    while parts:
        left = []
        for part, n in parts:
            for _ in range(n):
                if next(part, part) is part:
                    break
            else:
                left.append((part, n))
        parts = left


def finish(part):
    run([(part, 1)])


def turned(weight):
    return weight.astype(F32).T.astype(BF)


def store_halves(ref, at, values):
    ref[0, at, :] = values[:, :128]
    ref[1, at, :] = values[:, 128:]


def load_halves(ref, at):
    return jnp.concatenate([ref[0, at, :], ref[1, at, :]], axis=1)


def window_mix(xn, wk, weight):
    pairs = xn.shape[0] // 128
    wqv = jnp.concatenate([weight[:, :CH], weight[:, 2 * CH :]], axis=1)
    proj = nn(xn, wqv)
    query = (proj[:, :CH] * QSCALE).astype(BF)
    vals = proj[:, CH:].astype(BF)
    yield
    keys = nt(wk, xn).astype(BF)
    yield
    none = jnp.zeros((HEAD, 128), BF)
    lane = lax.broadcasted_iota(jnp.int32, (128, 128), 1)
    row = lax.broadcasted_iota(jnp.int32, (128, 128), 0)
    inside = jnp.where(lane == jnp.where(row < 64, 0, 1), 1.0, 0.0).astype(BF)
    across = (row == 0) & (lane >= 64) | (row == 1) & (lane < 64)
    across = jnp.where(across, -1e30, 0.0).astype(BF)

    def score(t, g):
        cols = []
        for j in range(4):
            h = 4 * g + j
            parts = [none] * 4
            parts[j] = keys[HEAD * h : HEAD * h + HEAD, 128 * t : 128 * t + 128]
            parts.append(across)
            cols.append(jnp.concatenate(parts, axis=0))
        left = query[128 * t : 128 * t + 128, 128 * g : 128 * g + 128]
        left = jnp.concatenate([left, inside], axis=1)
        return nn(left, jnp.concatenate(cols, axis=1))

    order = [(t, g) for t in range(pairs) for g in range(2)]
    ahead = [score(*order[n]) for n in range(WAHEAD)]
    mixed = []
    for n, (t, g) in enumerate(order):
        scores = ahead.pop(0)
        if n + WAHEAD < len(order):
            ahead.append(score(*order[n + WAHEAD]))
        v = vals[128 * t : 128 * t + 128, 128 * g : 128 * g + 128]
        probs = []
        right = []
        for j in range(4):
            part = scores[:, 128 * j : 128 * j + 128]
            top = jnp.max(part, axis=1, keepdims=True)
            probs.append(jnp.exp2(part - top).astype(BF))
            mask = (lane >= HEAD * j) & (lane < HEAD * j + HEAD)
            zero = jnp.zeros_like(v)
            right.append(
                jnp.concatenate(
                    [jnp.where(mask, v, zero), jnp.where(mask, jnp.ones_like(v), zero)], axis=1
                )
            )
        out = nn(jnp.concatenate(probs, axis=1), jnp.concatenate(right, axis=0))
        mixed.append((out[:, :128] / out[:, 128:]).astype(BF))
        yield
    return jnp.concatenate(
        [jnp.concatenate(mixed[2 * t : 2 * t + 2], axis=1) for t in range(pairs)], axis=0
    )


def grid_mix(xns, wk, weight):
    zq = jnp.zeros((HEAD, 256), BF)
    lane = lax.broadcasted_iota(jnp.int32, (256, 128), 1)
    wqv = jnp.concatenate([weight[:, :CH], weight[:, 2 * CH :]], axis=1)
    proj = [nn(xn, wqv) for xn in xns]
    keysT = [nt(wk, xn).astype(BF) for xn in xns]
    query = [(p[:, :CH] * QSCALE).astype(BF) for p in proj]
    vals = [p[:, CH:].astype(BF) for p in proj]

    def score(t, h):
        g, j = divmod(h, 4)
        parts = [zq] * 4
        parts[j] = keysT[t][HEAD * h : HEAD * h + HEAD]
        return nn(query[t][:, 128 * g : 128 * g + 128], jnp.concatenate(parts, axis=0))

    order = [(t, h) for h in range(HEADS) for t in range(len(xns))]
    ahead = [score(*order[n]) for n in range(AHEAD)]
    halves = [[] for _ in xns]
    acc = [None for _ in xns]
    for n, (t, h) in enumerate(order):
        g, j = divmod(h, 4)
        scores = ahead.pop(0)
        if n + AHEAD < len(order):
            ahead.append(score(*order[n + AHEAD]))
        top = jnp.max(scores, axis=1, keepdims=True)
        probs = jnp.exp2(scores - top).astype(BF)
        mask = (lane >= HEAD * j) & (lane < HEAD * j + HEAD)
        v = vals[t][:, 128 * g : 128 * g + 128]
        z = jnp.zeros_like(v)
        right = jnp.concatenate([jnp.where(mask, v, z), jnp.where(mask, jnp.ones_like(v), z)], axis=1)
        out = nn(probs, right)
        acc[t] = out if j == 0 else acc[t] + out
        if j == 3:
            halves[t].append((acc[t][:, :128] / acc[t][:, 128:]).astype(BF))
    return [jnp.concatenate(x, axis=1) for x in halves]


def front_kernel(
    edge_ref,
    image_ref,
    above_ref,
    below_ref,
    sides_ref,
    bn_gain_ref,
    bn_shift_ref,
    expand_ref,
    expand_bias_ref,
    depth_ref,
    depth_bias_ref,
    project_ref,
    gain_ref,
    qkv_ref,
    wo_ref,
    out_ref,
    line,
    hidden,
    side_hidden,
    middle,
    moved,
    wk,
    taps,
):
    step = pl.program_id(0)
    rows_dev = image_ref.shape[0]
    strips = rows_dev // WINDOW
    cell = lax.broadcasted_iota(jnp.int32, (16, 1), 0)

    def normed(values):
        return values.astype(F32) * (bn_gain_ref[...] * CUBE) + bn_shift_ref[...] * CUBE

    def activated(cells, c):
        lanes = slice(256 * c, 256 * c + 256)
        total = nn(cells, expand_ref[:, lanes]) + expand_bias_ref[:, lanes] * CUBE
        return scaled_gelu(total)

    def put(row, at, c, values):
        hidden[2 * c, row, at] = values[..., :128].astype(hidden.dtype)
        hidden[2 * c + 1, row, at] = values[..., 128:].astype(hidden.dtype)

    def expand_rows(rows, first_row, keep_at, keep):
        count = len(rows)
        for n in range(count):
            store_halves(line, slice(128 * n, 128 * n + 128), normed(rows[n]))
        cells = jnp.concatenate(
            [
                load_halves(line, pl.ds(128 * n + m, 16, stride=WINDOW))
                for n in range(count)
                for m in range(WINDOW)
            ],
            axis=0,
        ).astype(BF)
        for c in range(HID // 256):
            lanes = slice(256 * c, 256 * c + 256)
            act = activated(cells, c).reshape(count, WINDOW, 16, 256)
            yield
            for n in range(count):
                one = act[n] * keep if n == keep_at else act[n]
                row = first_row + n
                put(row, slice(1, WINDOW + 1), c, one)
                left = pltpu.roll(one[WINDOW - 1], 1, 0)
                right = pltpu.roll(one[0], 15, 0)
                left = jnp.where(cell == 0, side_hidden[pl.ds(row, 1), lanes], left)
                right = jnp.where(cell == 15, side_hidden[pl.ds(40 + row, 1), lanes], right)
                put(row, 0, c, left)
                put(row, WINDOW + 1, c, right)

    @pl.when(step == 0)
    def _():
        wk[...] = turned(qkv_ref[0, :, CH : 2 * CH])
        for tap in range(9):
            row = depth_ref[tap // 3, tap % 3 : tap % 3 + 1].astype(F32) * 0.5
            taps[8 * tap : 8 * tap + 8, :] = jnp.broadcast_to(row, (8, HID))
        taps[72:80, :] = jnp.broadcast_to(depth_bias_ref[...] * CUBE, (8, HID))
        cells = normed(sides_ref[...]).astype(BF)
        index = lax.broadcasted_iota(jnp.int32, (80, 1), 0)
        right = index >= 40
        row = jnp.where(right, index - 40, index)
        keep = jnp.where(right, edge_ref[3], edge_ref[2])
        keep = jnp.where(row == 0, keep * edge_ref[0], keep)
        keep = jnp.where(row == rows_dev + 1, keep * edge_ref[1], keep)
        keep = keep.astype(F32)
        for c in range(HID // 256):
            lanes = slice(256 * c, 256 * c + 256)
            side_hidden[:, lanes] = activated(cells, c) * keep
        finish(expand_rows([above_ref[...], image_ref[0]], 0, 0, edge_ref[0].astype(F32)))

    def expand(strip, i):
        base = strip * WINDOW + 1 + 4 * i
        rows = [image_ref[base + n] for n in range(3)]
        last = base + 3
        beyond = last == rows_dev
        final = image_ref[jnp.minimum(last, rows_dev - 1)]
        rows.append(jnp.where(beyond, below_ref[...], final))
        keep = jnp.where(beyond, edge_ref[1], 1).astype(F32)
        yield from expand_rows(rows, base + 1, 3, keep)

    def depth(strip, r):
        at = pl.ds(pl.multiple_of(r * 128, 128), 128)
        for c in range(HID // 128):
            lanes = slice(128 * c, 128 * c + 128)
            total = None
            for down in range(3):
                around = hidden[c, strip * WINDOW + r + down]
                around = around.reshape(WINDOW + 2, 2, 8, 128)
                for across in range(3):
                    tap = 8 * (3 * down + across)
                    term = around[across : across + WINDOW] * taps[tap : tap + 8, lanes]
                    total = term if total is None else total + term
            act = scaled_gelu(total + taps[72:80, lanes])
            middle[at, lanes] = act.reshape(128, 128).astype(BF)
            yield

    def project(i):
        for n in range(4):
            at = pl.ds(pl.multiple_of(512 * i + 128 * n, 128), 128)
            store_halves(moved, at, nn(middle[at, :], project_ref[...]) * (0.5 / CUBE))
            yield

    def windows(strip, i):
        pieces = []
        for p in range(4):
            col = pl.multiple_of(64 * i + 16 * p, 16)
            res = image_ref[pl.ds(strip * WINDOW, WINDOW), pl.ds(col, 16), :].astype(F32)
            res = res.reshape(WINDOW, 2, WINDOW, CH)
            for w in range(2):
                conv = load_halves(moved, pl.ds(2 * (4 * i + p) + w, 64, stride=16))
                pieces.append(res[:, w].reshape(64, CH) + conv)
        y = jnp.concatenate(pieces, axis=0)
        xn = normalised(y, gain_ref[0:1]).astype(BF)
        yield
        mixed = yield from window_mix(xn, wk[...], qkv_ref[0])
        y = (y + nn(mixed, wo_ref[0])).astype(BF)
        out_ref[0, :, :, i] = y.reshape(8, 4, 16, CH)

    def halves(*parts):
        def body(i, carry):
            run([(part(i), n) for part, n in parts])
            return carry

        lax.fori_loop(0, 2, body, 0)

    def depth_half(i):
        for n in range(4):
            yield from depth(step, 4 * i + n)

    def windows_half(i):
        return windows(step - 1, i)

    def expand_half(i):
        return expand(step + 1, i)

    @pl.when(step == 0)
    def _():
        halves((lambda i: expand(0, i), 1))
        halves((depth_half, 1))

    @pl.when((step > 0) & (step < strips))
    def _():
        halves((windows_half, 1), (depth_half, 3))

    @pl.when(step == strips)
    def _():
        halves((windows_half, 1))

    @pl.when(step < strips - 1)
    def _():
        halves((project, 1), (expand_half, 1))

    @pl.when(step == strips - 1)
    def _():
        halves((project, 1))


def grid_kernel(tokens_ref, gain_ref, qkv_ref, wo_ref, out_ref, work, wk):
    wk[...] = turned(qkv_ref[0, :, CH : 2 * CH])

    def norm_step(i, carry):
        at = pl.ds(pl.multiple_of(16 * i, 16), 16)
        y = tokens_ref[at].astype(F32).reshape(256, CH)
        rows = pl.ds(pl.multiple_of(256 * i, 256), 256)
        store_halves(work, rows, normalised(y, gain_ref[1:2]))
        return carry

    lax.fori_loop(0, 16, norm_step, 0)

    def set_step(k, carry):
        ats = [pl.ds(SETS * k + n, 256, stride=16) for n in range(SETS)]
        xns = [load_halves(work, at).astype(BF) for at in ats]
        mixed = grid_mix(xns, wk[...], qkv_ref[0])
        for n in range(SETS):
            store_halves(work, ats[n], nn(mixed[n], wo_ref[0]))
        return carry

    lax.fori_loop(0, 16 // SETS, set_step, 0)

    def add_step(i, carry):
        at = pl.ds(pl.multiple_of(16 * i, 16), 16)
        y = load_halves(work, pl.ds(pl.multiple_of(256 * i, 256), 256)).reshape(16, 16, CH)
        out_ref[at] = (tokens_ref[at].astype(F32) + y).astype(BF)
        return carry

    lax.fori_loop(0, 16, add_step, 0)


def whole(shape):
    return pl.BlockSpec(shape, lambda i: (0,) * len(shape))


def layer(shape, n):
    return pl.BlockSpec((1,) + shape[1:], lambda i: (n,) + (0,) * (len(shape) - 1))


def front(edge, image, above, below, sides, params):
    rows_dev, cols_dev, chans = image.shape
    strips = rows_dev // WINDOW
    args = (image, above, below, sides) + params
    return pl.pallas_call(
        front_kernel,
        grid=(strips + 1,),
        in_specs=[pl.BlockSpec(memory_space=pltpu.SMEM)]
        + [whole(a.shape) for a in args[:-2]]
        + [layer(a.shape, 0) for a in args[-2:]],
        out_specs=pl.BlockSpec(
            (1, 8, 4, 2, 16, chans), lambda i: (jnp.maximum(i - 1, 0), 0, 0, 0, 0, 0)
        ),
        out_shape=jax.ShapeDtypeStruct((strips, 8, 4, 2, 16, chans), BF),
        scratch_shapes=[
            pltpu.VMEM((2, 4 * cols_dev, 128), F32),
            pltpu.VMEM((HID // 128, rows_dev + 2, WINDOW + 2, 16, 128), F32),
            pltpu.VMEM((80, HID), F32),
            pltpu.VMEM((WINDOW * cols_dev, HID), BF),
            pltpu.VMEM((2, WINDOW * cols_dev, 128), F32),
            pltpu.VMEM((CH, CH), BF),
            pltpu.VMEM((80, HID), F32),
        ],
        compiler_params=pltpu.CompilerParams(
            dimension_semantics=("arbitrary",), vmem_limit_bytes=48 * 2**20
        ),
        name="front",
    )(edge, *args)


def grid_attention(tokens, gain, qkv, wo):
    return pl.pallas_call(
        grid_kernel,
        grid=(1,),
        in_specs=[whole(tokens.shape), whole(gain.shape), layer(qkv.shape, 1), layer(wo.shape, 1)],
        out_specs=whole(tokens.shape),
        out_shape=jax.ShapeDtypeStruct(tokens.shape, BF),
        scratch_shapes=[
            pltpu.VMEM((2, tokens.shape[0] * tokens.shape[1], 128), F32),
            pltpu.VMEM((CH, CH), BF),
        ],
        compiler_params=pltpu.CompilerParams(
            dimension_semantics=("arbitrary",), vmem_limit_bytes=40 * 2**20
        ),
        name="grid_attention",
    )(tokens, gain, qkv, wo)


def halos(image):
    rows = lax.axis_size("row")
    cols = lax.axis_size("col")
    up = [(i, i + 1) for i in range(rows - 1)]
    down = [(i + 1, i) for i in range(rows - 1)]
    above = lax.ppermute(image[-1:], "row", up)
    below = lax.ppermute(image[:1], "row", down)
    first = jnp.concatenate([above[:, :1], image[:, :1], below[:, :1]], axis=0)[:, 0]
    last = jnp.concatenate([above[:, -1:], image[:, -1:], below[:, -1:]], axis=0)[:, 0]
    left = lax.ppermute(last, "col", [(i, i + 1) for i in range(cols - 1)])
    right = lax.ppermute(first, "col", [(i + 1, i) for i in range(cols - 1)])
    pad = ((0, 40 - left.shape[0]), (0, 0))
    sides = jnp.concatenate([jnp.pad(left, pad), jnp.pad(right, pad)], axis=0)
    return above[0], below[0], sides


def per_device(
    image,
    bn_gain,
    bn_shift,
    expand_weight,
    expand_bias,
    depth_kernel,
    depth_bias,
    project_weight,
    norm_gain,
    qkv_weight,
    out_weight,
):
    rows_dev, cols_dev, chans = image.shape
    row_at = lax.axis_index("row")
    col_at = lax.axis_index("col")
    edge = jnp.stack(
        [
            row_at > 0,
            row_at < lax.axis_size("row") - 1,
            col_at > 0,
            col_at < lax.axis_size("col") - 1,
        ]
    ).astype(jnp.int32)
    above, below, sides = halos(image)
    params = (
        bn_gain[None],
        bn_shift[None],
        expand_weight,
        expand_bias[None],
        depth_kernel,
        depth_bias[None],
        project_weight,
        norm_gain,
        qkv_weight,
        out_weight,
    )
    after_block = front(edge, image, above, below, sides, params)
    outgoing = after_block.reshape(128, 32, chans)
    received = lax.all_to_all(outgoing, ("row", "col"), split_axis=0, concat_axis=0, tiled=True)
    done = grid_attention(received.reshape(256, 16, chans), norm_gain, qkv_weight, out_weight)
    returned = lax.all_to_all(
        done.reshape(128, 32, chans), ("row", "col"), split_axis=0, concat_axis=0, tiled=True
    )
    placed = returned.reshape(4, 8, 4, 2, 2, 8, chans).transpose(0, 2, 4, 3, 1, 5, 6)
    return placed.reshape(rows_dev, cols_dev, chans)


def solution(mesh):
    in_specs = (P("row", "col", None), P(), P(), P(), P(), P(), P(), P(), P(), P(), P())
    out_specs = P("row", "col", None)
    return jax.shard_map(
        per_device, mesh=mesh, in_specs=in_specs, out_specs=out_specs, check_vma=False
    )
```

```python
import jax
import jax.numpy as jnp
from jax import lax
from jax.experimental import pallas as pl
from jax.experimental.pallas import tpu as pltpu
from jax.sharding import PartitionSpec as P

HEADS = 8
SETS = 4
AHEAD = 4
WAHEAD = 2


HEAD = 32
CH = 256
HID = 1024
WINDOW = 8
EPS = 1e-5
GELU_A = 0.7978845608028654
CUBE = (GELU_A * 0.044715) ** (1.0 / 3.0)
GELU_C = GELU_A / CUBE
QSCALE = 32.0**-0.5 * 1.4426950408889634
BF = jnp.bfloat16
F32 = jnp.float32


def mm(a, b, dims):
    return lax.dot_general(a, b, (dims, ((), ())), preferred_element_type=F32)


def nn(a, b):
    return mm(a, b, ((1,), (0,)))


def nt(a, b):
    return mm(a, b, ((1,), (1,)))


def tn(a, b):
    return mm(a, b, ((0,), (0,)))


def scaled_gelu(z):
    return z + z * jnp.tanh(z * (z * z + GELU_C))


def normalised(y, gain):
    mean = jnp.mean(y, axis=-1, keepdims=True)
    centred = y - mean
    spread = jnp.mean(centred * centred, axis=-1, keepdims=True)
    return centred * lax.rsqrt(spread + EPS) * gain


def run(parts):
    while parts:
        left = []
        for part, n in parts:
            for _ in range(n):
                if next(part, part) is part:
                    break
            else:
                left.append((part, n))
        parts = left


def finish(part):
    run([(part, 1)])


def turned(weight):
    return weight.astype(F32).T.astype(BF)


def store_halves(ref, at, values):
    ref[0, at, :] = values[:, :128]
    ref[1, at, :] = values[:, 128:]


def load_halves(ref, at):
    return jnp.concatenate([ref[0, at, :], ref[1, at, :]], axis=1)


def window_mix(xn, wk, weight):
    pairs = xn.shape[0] // 128
    wqv = jnp.concatenate([weight[:, :CH], weight[:, 2 * CH :]], axis=1)
    proj = nn(xn, wqv)
    query = (proj[:, :CH] * QSCALE).astype(BF)
    vals = proj[:, CH:].astype(BF)
    yield
    keys = nt(wk, xn).astype(BF)
    yield
    none = jnp.zeros((HEAD, 128), BF)
    lane = lax.broadcasted_iota(jnp.int32, (128, 128), 1)
    row = lax.broadcasted_iota(jnp.int32, (128, 128), 0)
    inside = jnp.where(lane == jnp.where(row < 64, 0, 1), 1.0, 0.0).astype(BF)
    across = (row == 0) & (lane >= 64) | (row == 1) & (lane < 64)
    across = jnp.where(across, -1e30, 0.0).astype(BF)

    def score(t, g):
        cols = []
        for j in range(4):
            h = 4 * g + j
            parts = [none] * 4
            parts[j] = keys[HEAD * h : HEAD * h + HEAD, 128 * t : 128 * t + 128]
            parts.append(across)
            cols.append(jnp.concatenate(parts, axis=0))
        left = query[128 * t : 128 * t + 128, 128 * g : 128 * g + 128]
        left = jnp.concatenate([left, inside], axis=1)
        return nn(left, jnp.concatenate(cols, axis=1))

    order = [(t, g) for t in range(pairs) for g in range(2)]
    ahead = [score(*order[n]) for n in range(WAHEAD)]
    mixed = []
    for n, (t, g) in enumerate(order):
        scores = ahead.pop(0)
        if n + WAHEAD < len(order):
            ahead.append(score(*order[n + WAHEAD]))
        v = vals[128 * t : 128 * t + 128, 128 * g : 128 * g + 128]
        probs = []
        right = []
        for j in range(4):
            part = scores[:, 128 * j : 128 * j + 128]
            top = jnp.max(part, axis=1, keepdims=True)
            probs.append(jnp.exp2(part - top).astype(BF))
            mask = (lane >= HEAD * j) & (lane < HEAD * j + HEAD)
            zero = jnp.zeros_like(v)
            right.append(
                jnp.concatenate(
                    [jnp.where(mask, v, zero), jnp.where(mask, jnp.ones_like(v), zero)], axis=1
                )
            )
        out = nn(jnp.concatenate(probs, axis=1), jnp.concatenate(right, axis=0))
        mixed.append((out[:, :128] / out[:, 128:]).astype(BF))
        yield
    return jnp.concatenate(
        [jnp.concatenate(mixed[2 * t : 2 * t + 2], axis=1) for t in range(pairs)], axis=0
    )


def grid_mix(xns, wk, weight):
    zq = jnp.zeros((HEAD, 256), BF)
    lane = lax.broadcasted_iota(jnp.int32, (256, 128), 1)
    wqv = jnp.concatenate([weight[:, :CH], weight[:, 2 * CH :]], axis=1)
    proj = [nn(xn, wqv) for xn in xns]
    keysT = [nt(wk, xn).astype(BF) for xn in xns]
    query = [(p[:, :CH] * QSCALE).astype(BF) for p in proj]
    vals = [p[:, CH:].astype(BF) for p in proj]

    def score(t, h):
        g, j = divmod(h, 4)
        parts = [zq] * 4
        parts[j] = keysT[t][HEAD * h : HEAD * h + HEAD]
        return nn(query[t][:, 128 * g : 128 * g + 128], jnp.concatenate(parts, axis=0))

    order = [(t, h) for h in range(HEADS) for t in range(len(xns))]
    ahead = [score(*order[n]) for n in range(AHEAD)]
    halves = [[] for _ in xns]
    acc = [None for _ in xns]
    for n, (t, h) in enumerate(order):
        g, j = divmod(h, 4)
        scores = ahead.pop(0)
        if n + AHEAD < len(order):
            ahead.append(score(*order[n + AHEAD]))
        top = jnp.max(scores, axis=1, keepdims=True)
        probs = jnp.exp2(scores - top).astype(BF)
        mask = (lane >= HEAD * j) & (lane < HEAD * j + HEAD)
        v = vals[t][:, 128 * g : 128 * g + 128]
        z = jnp.zeros_like(v)
        right = jnp.concatenate([jnp.where(mask, v, z), jnp.where(mask, jnp.ones_like(v), z)], axis=1)
        out = nn(probs, right)
        acc[t] = out if j == 0 else acc[t] + out
        if j == 3:
            halves[t].append((acc[t][:, :128] / acc[t][:, 128:]).astype(BF))
    return [jnp.concatenate(x, axis=1) for x in halves]


def front_kernel(
    edge_ref,
    image_ref,
    above_ref,
    below_ref,
    sides_ref,
    bn_gain_ref,
    bn_shift_ref,
    expand_ref,
    expand_bias_ref,
    depth_ref,
    depth_bias_ref,
    project_ref,
    gain_ref,
    qkv_ref,
    wo_ref,
    out_ref,
    line,
    hidden,
    side_hidden,
    middle,
    moved,
    wk,
    taps,
):
    step = pl.program_id(0)
    rows_dev = image_ref.shape[0]
    strips = rows_dev // WINDOW
    cell = lax.broadcasted_iota(jnp.int32, (16, 1), 0)

    def normed(values):
        return values.astype(F32) * (bn_gain_ref[...] * CUBE) + bn_shift_ref[...] * CUBE

    def activated(cells, c):
        lanes = slice(256 * c, 256 * c + 256)
        total = nn(cells, expand_ref[:, lanes]) + expand_bias_ref[:, lanes] * CUBE
        return scaled_gelu(total)

    def put(row, at, c, values):
        hidden[2 * c, row, at] = values[..., :128].astype(hidden.dtype)
        hidden[2 * c + 1, row, at] = values[..., 128:].astype(hidden.dtype)

    def expand_rows(rows, first_row, keep_at, keep):
        count = len(rows)
        for n in range(count):
            store_halves(line, slice(128 * n, 128 * n + 128), normed(rows[n]))
        cells = jnp.concatenate(
            [
                load_halves(line, pl.ds(128 * n + m, 16, stride=WINDOW))
                for n in range(count)
                for m in range(WINDOW)
            ],
            axis=0,
        ).astype(BF)
        for c in range(HID // 256):
            lanes = slice(256 * c, 256 * c + 256)
            act = activated(cells, c).reshape(count, WINDOW, 16, 256)
            yield
            for n in range(count):
                one = act[n] * keep if n == keep_at else act[n]
                row = first_row + n
                put(row, slice(1, WINDOW + 1), c, one)
                left = pltpu.roll(one[WINDOW - 1], 1, 0)
                right = pltpu.roll(one[0], 15, 0)
                left = jnp.where(cell == 0, side_hidden[pl.ds(row, 1), lanes], left)
                right = jnp.where(cell == 15, side_hidden[pl.ds(40 + row, 1), lanes], right)
                put(row, 0, c, left)
                put(row, WINDOW + 1, c, right)

    @pl.when(step == 0)
    def _():
        wk[...] = turned(qkv_ref[0, :, CH : 2 * CH])
        for tap in range(9):
            row = depth_ref[tap // 3, tap % 3 : tap % 3 + 1].astype(F32) * 0.5
            taps[8 * tap : 8 * tap + 8, :] = jnp.broadcast_to(row, (8, HID))
        taps[72:80, :] = jnp.broadcast_to(depth_bias_ref[...] * CUBE, (8, HID))
        cells = normed(sides_ref[...]).astype(BF)
        index = lax.broadcasted_iota(jnp.int32, (80, 1), 0)
        right = index >= 40
        row = jnp.where(right, index - 40, index)
        keep = jnp.where(right, edge_ref[3], edge_ref[2])
        keep = jnp.where(row == 0, keep * edge_ref[0], keep)
        keep = jnp.where(row == rows_dev + 1, keep * edge_ref[1], keep)
        keep = keep.astype(F32)
        for c in range(HID // 256):
            lanes = slice(256 * c, 256 * c + 256)
            side_hidden[:, lanes] = activated(cells, c) * keep
        finish(expand_rows([above_ref[...], image_ref[0]], 0, 0, edge_ref[0].astype(F32)))

    def expand(strip, i):
        base = strip * WINDOW + 1 + 4 * i
        rows = [image_ref[base + n] for n in range(3)]
        last = base + 3
        beyond = last == rows_dev
        final = image_ref[jnp.minimum(last, rows_dev - 1)]
        rows.append(jnp.where(beyond, below_ref[...], final))
        keep = jnp.where(beyond, edge_ref[1], 1).astype(F32)
        yield from expand_rows(rows, base + 1, 3, keep)

    def depth(strip, r):
        at = pl.ds(pl.multiple_of(r * 128, 128), 128)
        for c in range(HID // 128):
            lanes = slice(128 * c, 128 * c + 128)
            total = None
            for down in range(3):
                around = hidden[c, strip * WINDOW + r + down]
                around = around.reshape(WINDOW + 2, 2, 8, 128)
                for across in range(3):
                    tap = 8 * (3 * down + across)
                    term = around[across : across + WINDOW] * taps[tap : tap + 8, lanes]
                    total = term if total is None else total + term
            act = scaled_gelu(total + taps[72:80, lanes])
            middle[at, lanes] = act.reshape(128, 128).astype(BF)
            yield

    def project(i):
        for n in range(4):
            at = pl.ds(pl.multiple_of(512 * i + 128 * n, 128), 128)
            store_halves(moved, at, nn(middle[at, :], project_ref[...]) * (0.5 / CUBE))
            yield

    def windows(strip, i):
        pieces = []
        for p in range(4):
            col = pl.multiple_of(64 * i + 16 * p, 16)
            res = image_ref[pl.ds(strip * WINDOW, WINDOW), pl.ds(col, 16), :].astype(F32)
            res = res.reshape(WINDOW, 2, WINDOW, CH)
            for w in range(2):
                conv = load_halves(moved, pl.ds(2 * (4 * i + p) + w, 64, stride=16))
                pieces.append(res[:, w].reshape(64, CH) + conv)
        y = jnp.concatenate(pieces, axis=0)
        xn = normalised(y, gain_ref[0:1]).astype(BF)
        yield
        mixed = yield from window_mix(xn, wk[...], qkv_ref[0])
        y = (y + nn(mixed, wo_ref[0])).astype(BF)
        out_ref[0, :, :, i] = y.reshape(8, 4, 16, CH)

    def halves(*parts):
        def body(i, carry):
            run([(part(i), n) for part, n in parts])
            return carry

        lax.fori_loop(0, 2, body, 0)

    def depth_half(i):
        for n in range(4):
            yield from depth(step, 4 * i + n)

    def windows_half(i):
        return windows(step - 1, i)

    def expand_half(i):
        return expand(step + 1, i)

    @pl.when(step == 0)
    def _():
        halves((lambda i: expand(0, i), 1))
        halves((depth_half, 1))

    @pl.when((step > 0) & (step < strips))
    def _():
        halves((windows_half, 1), (depth_half, 3))

    @pl.when(step == strips)
    def _():
        halves((windows_half, 1))

    @pl.when(step < strips - 1)
    def _():
        halves((project, 1), (expand_half, 1))

    @pl.when(step == strips - 1)
    def _():
        halves((project, 1))


def grid_kernel(tokens_ref, gain_ref, qkv_ref, wo_ref, out_ref, work, wk):
    wk[...] = turned(qkv_ref[0, :, CH : 2 * CH])

    def spread_step(i, carry):
        at = pl.ds(pl.multiple_of(16 * i, 16), 16)
        y = tokens_ref[at].astype(F32).reshape(256, CH)
        store_halves(work, pl.ds(pl.multiple_of(256 * i, 256), 256), y)
        return carry

    lax.fori_loop(0, 16, spread_step, 0)

    def set_step(k, carry):
        ats = [pl.ds(SETS * k + n, 256, stride=16) for n in range(SETS)]
        xns = [normalised(load_halves(work, at), gain_ref[1:2]).astype(BF) for at in ats]
        mixed = grid_mix(xns, wk[...], qkv_ref[0])
        for n in range(SETS):
            store_halves(work, ats[n], load_halves(work, ats[n]) + nn(mixed[n], wo_ref[0]))
        return carry

    lax.fori_loop(0, 16 // SETS, set_step, 0)

    def collect_step(i, carry):
        at = pl.ds(pl.multiple_of(16 * i, 16), 16)
        y = load_halves(work, pl.ds(pl.multiple_of(256 * i, 256), 256))
        out_ref[at] = y.reshape(16, 16, CH).astype(BF)
        return carry

    lax.fori_loop(0, 16, collect_step, 0)


def whole(shape):
    return pl.BlockSpec(shape, lambda i: (0,) * len(shape))


def layer(shape, n):
    return pl.BlockSpec((1,) + shape[1:], lambda i: (n,) + (0,) * (len(shape) - 1))


def front(edge, image, above, below, sides, params):
    rows_dev, cols_dev, chans = image.shape
    strips = rows_dev // WINDOW
    args = (image, above, below, sides) + params
    return pl.pallas_call(
        front_kernel,
        grid=(strips + 1,),
        in_specs=[pl.BlockSpec(memory_space=pltpu.SMEM)]
        + [whole(a.shape) for a in args[:-2]]
        + [layer(a.shape, 0) for a in args[-2:]],
        out_specs=pl.BlockSpec(
            (1, 8, 4, 2, 16, chans), lambda i: (jnp.maximum(i - 1, 0), 0, 0, 0, 0, 0)
        ),
        out_shape=jax.ShapeDtypeStruct((strips, 8, 4, 2, 16, chans), BF),
        scratch_shapes=[
            pltpu.VMEM((2, 4 * cols_dev, 128), F32),
            pltpu.VMEM((HID // 128, rows_dev + 2, WINDOW + 2, 16, 128), F32),
            pltpu.VMEM((80, HID), F32),
            pltpu.VMEM((WINDOW * cols_dev, HID), BF),
            pltpu.VMEM((2, WINDOW * cols_dev, 128), F32),
            pltpu.VMEM((CH, CH), BF),
            pltpu.VMEM((80, HID), F32),
        ],
        compiler_params=pltpu.CompilerParams(
            dimension_semantics=("arbitrary",), vmem_limit_bytes=60 * 2**20
        ),
        name="front",
    )(edge, *args)


def grid_attention(tokens, gain, qkv, wo):
    return pl.pallas_call(
        grid_kernel,
        grid=(1,),
        in_specs=[whole(tokens.shape), whole(gain.shape), layer(qkv.shape, 1), layer(wo.shape, 1)],
        out_specs=whole(tokens.shape),
        out_shape=jax.ShapeDtypeStruct(tokens.shape, BF),
        scratch_shapes=[
            pltpu.VMEM((2, tokens.shape[0] * tokens.shape[1], 128), F32),
            pltpu.VMEM((CH, CH), BF),
        ],
        compiler_params=pltpu.CompilerParams(
            dimension_semantics=("arbitrary",), vmem_limit_bytes=40 * 2**20
        ),
        name="grid_attention",
    )(tokens, gain, qkv, wo)


def halos(image):
    rows = lax.axis_size("row")
    cols = lax.axis_size("col")
    up = [(i, i + 1) for i in range(rows - 1)]
    down = [(i + 1, i) for i in range(rows - 1)]
    above = lax.ppermute(image[-1:], "row", up)
    below = lax.ppermute(image[:1], "row", down)
    first = jnp.concatenate([above[:, :1], image[:, :1], below[:, :1]], axis=0)[:, 0]
    last = jnp.concatenate([above[:, -1:], image[:, -1:], below[:, -1:]], axis=0)[:, 0]
    left = lax.ppermute(last, "col", [(i, i + 1) for i in range(cols - 1)])
    right = lax.ppermute(first, "col", [(i + 1, i) for i in range(cols - 1)])
    pad = ((0, 40 - left.shape[0]), (0, 0))
    sides = jnp.concatenate([jnp.pad(left, pad), jnp.pad(right, pad)], axis=0)
    return above[0], below[0], sides


def per_device(
    image,
    bn_gain,
    bn_shift,
    expand_weight,
    expand_bias,
    depth_kernel,
    depth_bias,
    project_weight,
    norm_gain,
    qkv_weight,
    out_weight,
):
    rows_dev, cols_dev, chans = image.shape
    row_at = lax.axis_index("row")
    col_at = lax.axis_index("col")
    edge = jnp.stack(
        [
            row_at > 0,
            row_at < lax.axis_size("row") - 1,
            col_at > 0,
            col_at < lax.axis_size("col") - 1,
        ]
    ).astype(jnp.int32)
    above, below, sides = halos(image)
    params = (
        bn_gain[None],
        bn_shift[None],
        expand_weight,
        expand_bias[None],
        depth_kernel,
        depth_bias[None],
        project_weight,
        norm_gain,
        qkv_weight,
        out_weight,
    )
    after_block = front(edge, image, above, below, sides, params)
    outgoing = after_block.reshape(128, 32, chans)
    received = lax.all_to_all(outgoing, ("row", "col"), split_axis=0, concat_axis=0, tiled=True)
    done = grid_attention(received.reshape(256, 16, chans), norm_gain, qkv_weight, out_weight)
    returned = lax.all_to_all(
        done.reshape(128, 32, chans), ("row", "col"), split_axis=0, concat_axis=0, tiled=True
    )
    placed = returned.reshape(4, 8, 4, 2, 2, 8, chans).transpose(0, 2, 4, 3, 1, 5, 6)
    return placed.reshape(rows_dev, cols_dev, chans)


def solution(mesh):
    in_specs = (P("row", "col", None), P(), P(), P(), P(), P(), P(), P(), P(), P(), P())
    out_specs = P("row", "col", None)
    return jax.shard_map(
        per_device, mesh=mesh, in_specs=in_specs, out_specs=out_specs, check_vma=False
    )
```

```python
import jax
import jax.numpy as jnp
from jax import lax
from jax.experimental import pallas as pl
from jax.experimental.pallas import tpu as pltpu
from jax.sharding import PartitionSpec as P

HEADS = 8
SETS = 4
AHEAD = 4
WAHEAD = 2


HEAD = 32
CH = 256
HID = 1024
WINDOW = 8
EPS = 1e-5
GELU_A = 0.7978845608028654
CUBE = (GELU_A * 0.044715) ** (1.0 / 3.0)
GELU_C = GELU_A / CUBE
QSCALE = 32.0**-0.5 * 1.4426950408889634
BF = jnp.bfloat16
F32 = jnp.float32


def mm(a, b, dims):
    return lax.dot_general(a, b, (dims, ((), ())), preferred_element_type=F32)


def nn(a, b):
    return mm(a, b, ((1,), (0,)))


def nt(a, b):
    return mm(a, b, ((1,), (1,)))


def tn(a, b):
    return mm(a, b, ((0,), (0,)))


def scaled_gelu(z):
    return z + z * jnp.tanh(z * (z * z + GELU_C))


def normalised(y, gain):
    mean = jnp.mean(y, axis=-1, keepdims=True)
    centred = y - mean
    spread = jnp.mean(centred * centred, axis=-1, keepdims=True)
    return centred * lax.rsqrt(spread + EPS) * gain


def run(parts):
    while parts:
        left = []
        for part, n in parts:
            for _ in range(n):
                if next(part, part) is part:
                    break
            else:
                left.append((part, n))
        parts = left


def finish(part):
    run([(part, 1)])


def turned(weight):
    return weight.astype(F32).T.astype(BF)


def store_halves(ref, at, values):
    ref[0, at, :] = values[:, :128]
    ref[1, at, :] = values[:, 128:]


def load_halves(ref, at):
    return jnp.concatenate([ref[0, at, :], ref[1, at, :]], axis=1)


def window_mix(xn, wk, weight):
    pairs = xn.shape[0] // 128
    wqv = jnp.concatenate([weight[:, :CH], weight[:, 2 * CH :]], axis=1)
    proj = nn(xn, wqv)
    query = (proj[:, :CH] * QSCALE).astype(BF)
    vals = proj[:, CH:].astype(BF)
    yield
    keys = nt(wk, xn).astype(BF)
    yield
    none = jnp.zeros((HEAD, 128), BF)
    lane = lax.broadcasted_iota(jnp.int32, (128, 128), 1)
    row = lax.broadcasted_iota(jnp.int32, (128, 128), 0)
    inside = jnp.where(lane == jnp.where(row < 64, 0, 1), 1.0, 0.0).astype(BF)
    across = (row == 0) & (lane >= 64) | (row == 1) & (lane < 64)
    across = jnp.where(across, -1e30, 0.0).astype(BF)

    def score(t, g):
        cols = []
        for j in range(4):
            h = 4 * g + j
            parts = [none] * 4
            parts[j] = keys[HEAD * h : HEAD * h + HEAD, 128 * t : 128 * t + 128]
            parts.append(across)
            cols.append(jnp.concatenate(parts, axis=0))
        left = query[128 * t : 128 * t + 128, 128 * g : 128 * g + 128]
        left = jnp.concatenate([left, inside], axis=1)
        return nn(left, jnp.concatenate(cols, axis=1))

    order = [(t, g) for t in range(pairs) for g in range(2)]
    ahead = [score(*order[n]) for n in range(WAHEAD)]
    mixed = []
    for n, (t, g) in enumerate(order):
        scores = ahead.pop(0)
        if n + WAHEAD < len(order):
            ahead.append(score(*order[n + WAHEAD]))
        v = vals[128 * t : 128 * t + 128, 128 * g : 128 * g + 128]
        probs = []
        right = []
        for j in range(4):
            part = scores[:, 128 * j : 128 * j + 128]
            top = jnp.max(part, axis=1, keepdims=True)
            probs.append(jnp.exp2(part - top).astype(BF))
            mask = (lane >= HEAD * j) & (lane < HEAD * j + HEAD)
            zero = jnp.zeros_like(v)
            right.append(
                jnp.concatenate(
                    [jnp.where(mask, v, zero), jnp.where(mask, jnp.ones_like(v), zero)], axis=1
                )
            )
        out = nn(jnp.concatenate(probs, axis=1), jnp.concatenate(right, axis=0))
        mixed.append((out[:, :128] / out[:, 128:]).astype(BF))
        yield
    return jnp.concatenate(
        [jnp.concatenate(mixed[2 * t : 2 * t + 2], axis=1) for t in range(pairs)], axis=0
    )


def grid_mix(xns, wk, weight):
    zq = jnp.zeros((HEAD, 256), BF)
    lane = lax.broadcasted_iota(jnp.int32, (256, 128), 1)
    wqv = jnp.concatenate([weight[:, :CH], weight[:, 2 * CH :]], axis=1)
    proj = [nn(xn, wqv) for xn in xns]
    keysT = [nt(wk, xn).astype(BF) for xn in xns]
    query = [(p[:, :CH] * QSCALE).astype(BF) for p in proj]
    vals = [p[:, CH:].astype(BF) for p in proj]

    def score(t, h):
        g, j = divmod(h, 4)
        parts = [zq] * 4
        parts[j] = keysT[t][HEAD * h : HEAD * h + HEAD]
        return nn(query[t][:, 128 * g : 128 * g + 128], jnp.concatenate(parts, axis=0))

    order = [(t, h) for h in range(HEADS) for t in range(len(xns))]
    ahead = [score(*order[n]) for n in range(AHEAD)]
    halves = [[] for _ in xns]
    acc = [None for _ in xns]
    for n, (t, h) in enumerate(order):
        g, j = divmod(h, 4)
        scores = ahead.pop(0)
        if n + AHEAD < len(order):
            ahead.append(score(*order[n + AHEAD]))
        top = jnp.max(scores, axis=1, keepdims=True)
        probs = jnp.exp2(scores - top).astype(BF)
        mask = (lane >= HEAD * j) & (lane < HEAD * j + HEAD)
        v = vals[t][:, 128 * g : 128 * g + 128]
        z = jnp.zeros_like(v)
        right = jnp.concatenate([jnp.where(mask, v, z), jnp.where(mask, jnp.ones_like(v), z)], axis=1)
        out = nn(probs, right)
        acc[t] = out if j == 0 else acc[t] + out
        if j == 3:
            halves[t].append((acc[t][:, :128] / acc[t][:, 128:]).astype(BF))
    return [jnp.concatenate(x, axis=1) for x in halves]


def front_kernel(
    edge_ref,
    image_ref,
    above_ref,
    below_ref,
    left_ref,
    right_ref,
    bn_gain_ref,
    bn_shift_ref,
    expand_ref,
    expand_bias_ref,
    depth_ref,
    depth_bias_ref,
    project_ref,
    gain_ref,
    qkv_ref,
    wo_ref,
    out_ref,
    line,
    hidden,
    side_hidden,
    middle,
    moved,
    wk,
    taps,
):
    step = pl.program_id(0)
    rows_dev = image_ref.shape[0]
    strips = rows_dev // WINDOW
    cell = lax.broadcasted_iota(jnp.int32, (16, 1), 0)

    def normed(values):
        return values.astype(F32) * (bn_gain_ref[...] * CUBE) + bn_shift_ref[...] * CUBE

    def activated(cells, c):
        lanes = slice(256 * c, 256 * c + 256)
        total = nn(cells, expand_ref[:, lanes]) + expand_bias_ref[:, lanes] * CUBE
        return scaled_gelu(total)

    def put(row, at, c, values):
        hidden[2 * c, row, at] = values[..., :128].astype(hidden.dtype)
        hidden[2 * c + 1, row, at] = values[..., 128:].astype(hidden.dtype)

    def expand_rows(rows, first_row, keep_at, keep):
        count = len(rows)
        for n in range(count):
            store_halves(line, slice(128 * n, 128 * n + 128), normed(rows[n]))
        cells = jnp.concatenate(
            [
                load_halves(line, pl.ds(128 * n + m, 16, stride=WINDOW))
                for n in range(count)
                for m in range(WINDOW)
            ],
            axis=0,
        ).astype(BF)
        for c in range(HID // 256):
            lanes = slice(256 * c, 256 * c + 256)
            act = activated(cells, c).reshape(count, WINDOW, 16, 256)
            yield
            for n in range(count):
                one = act[n] * keep if n == keep_at else act[n]
                row = first_row + n
                put(row, slice(1, WINDOW + 1), c, one)
                left = pltpu.roll(one[WINDOW - 1], 1, 0)
                right = pltpu.roll(one[0], 15, 0)
                left = jnp.where(cell == 0, side_hidden[pl.ds(row, 1), lanes], left)
                right = jnp.where(cell == 15, side_hidden[pl.ds(40 + row, 1), lanes], right)
                put(row, 0, c, left)
                put(row, WINDOW + 1, c, right)

    @pl.when(step == 0)
    def _():
        wk[...] = turned(qkv_ref[0, :, CH : 2 * CH])
        for tap in range(9):
            row = depth_ref[tap // 3, tap % 3 : tap % 3 + 1].astype(F32) * 0.5
            taps[8 * tap : 8 * tap + 8, :] = jnp.broadcast_to(row, (8, HID))
        taps[72:80, :] = jnp.broadcast_to(depth_bias_ref[...] * CUBE, (8, HID))
        cells = jnp.concatenate([normed(left_ref[...]), normed(right_ref[...])], axis=0).astype(BF)
        index = lax.broadcasted_iota(jnp.int32, (80, 1), 0)
        right = index >= 40
        row = jnp.where(right, index - 40, index)
        keep = jnp.where(right, edge_ref[3], edge_ref[2])
        keep = jnp.where(row == 0, keep * edge_ref[0], keep)
        keep = jnp.where(row == rows_dev + 1, keep * edge_ref[1], keep)
        keep = keep.astype(F32)
        for c in range(HID // 256):
            lanes = slice(256 * c, 256 * c + 256)
            side_hidden[:, lanes] = activated(cells, c) * keep
        finish(expand_rows([above_ref[...], image_ref[0]], 0, 0, edge_ref[0].astype(F32)))

    def expand(strip, i):
        base = strip * WINDOW + 1 + 4 * i
        rows = [image_ref[base + n] for n in range(3)]
        last = base + 3
        beyond = last == rows_dev
        final = image_ref[jnp.minimum(last, rows_dev - 1)]
        rows.append(jnp.where(beyond, below_ref[...], final))
        keep = jnp.where(beyond, edge_ref[1], 1).astype(F32)
        yield from expand_rows(rows, base + 1, 3, keep)

    def depth(strip, r):
        at = pl.ds(pl.multiple_of(r * 128, 128), 128)
        for c in range(HID // 128):
            lanes = slice(128 * c, 128 * c + 128)
            total = None
            for down in range(3):
                around = hidden[c, strip * WINDOW + r + down]
                around = around.reshape(WINDOW + 2, 2, 8, 128)
                for across in range(3):
                    tap = 8 * (3 * down + across)
                    term = around[across : across + WINDOW] * taps[tap : tap + 8, lanes]
                    total = term if total is None else total + term
            act = scaled_gelu(total + taps[72:80, lanes])
            middle[at, lanes] = act.reshape(128, 128).astype(BF)
            yield

    def project(i):
        for n in range(4):
            at = pl.ds(pl.multiple_of(512 * i + 128 * n, 128), 128)
            store_halves(moved, at, nn(middle[at, :], project_ref[...]) * (0.5 / CUBE))
            yield

    def windows(strip, i):
        pieces = []
        for p in range(4):
            col = pl.multiple_of(64 * i + 16 * p, 16)
            res = image_ref[pl.ds(strip * WINDOW, WINDOW), pl.ds(col, 16), :].astype(F32)
            res = res.reshape(WINDOW, 2, WINDOW, CH)
            for w in range(2):
                conv = load_halves(moved, pl.ds(2 * (4 * i + p) + w, 64, stride=16))
                pieces.append(res[:, w].reshape(64, CH) + conv)
        y = jnp.concatenate(pieces, axis=0)
        xn = normalised(y, gain_ref[0:1]).astype(BF)
        yield
        mixed = yield from window_mix(xn, wk[...], qkv_ref[0])
        y = (y + nn(mixed, wo_ref[0])).astype(BF)
        out_ref[0, :, :, i] = y.reshape(8, 4, 16, CH)

    def halves(*parts):
        def body(i, carry):
            run([(part(i), n) for part, n in parts])
            return carry

        lax.fori_loop(0, 2, body, 0)

    def depth_half(i):
        for n in range(4):
            yield from depth(step, 4 * i + n)

    def windows_half(i):
        return windows(step - 1, i)

    def expand_half(i):
        return expand(step + 1, i)

    @pl.when(step == 0)
    def _():
        halves((lambda i: expand(0, i), 1))
        halves((depth_half, 1))

    @pl.when((step > 0) & (step < strips))
    def _():
        halves((windows_half, 1), (depth_half, 3))

    @pl.when(step == strips)
    def _():
        halves((windows_half, 1))

    @pl.when(step < strips - 1)
    def _():
        halves((project, 1), (expand_half, 1))

    @pl.when(step == strips - 1)
    def _():
        halves((project, 1))


def grid_kernel(tokens_ref, gain_ref, qkv_ref, wo_ref, out_ref, work, wk):
    wk[...] = turned(qkv_ref[0, :, CH : 2 * CH])

    def spread_step(i, carry):
        at = pl.ds(pl.multiple_of(16 * i, 16), 16)
        y = tokens_ref[at].astype(F32).reshape(256, CH)
        store_halves(work, pl.ds(pl.multiple_of(256 * i, 256), 256), y)
        return carry

    lax.fori_loop(0, 16, spread_step, 0)

    def set_step(k, carry):
        ats = [pl.ds(SETS * k + n, 256, stride=16) for n in range(SETS)]
        xns = [normalised(load_halves(work, at), gain_ref[1:2]).astype(BF) for at in ats]
        mixed = grid_mix(xns, wk[...], qkv_ref[0])
        for n in range(SETS):
            store_halves(work, ats[n], load_halves(work, ats[n]) + nn(mixed[n], wo_ref[0]))
        return carry

    lax.fori_loop(0, 16 // SETS, set_step, 0)

    def collect_step(i, carry):
        at = pl.ds(pl.multiple_of(16 * i, 16), 16)
        y = load_halves(work, pl.ds(pl.multiple_of(256 * i, 256), 256))
        out_ref[at] = y.reshape(16, 16, CH).astype(BF)
        return carry

    lax.fori_loop(0, 16, collect_step, 0)


def whole(shape):
    return pl.BlockSpec(shape, lambda i: (0,) * len(shape))


def layer(shape, n):
    return pl.BlockSpec((1,) + shape[1:], lambda i: (n,) + (0,) * (len(shape) - 1))


def front(edge, image, above, below, left, right, params):
    rows_dev, cols_dev, chans = image.shape
    strips = rows_dev // WINDOW
    args = (image, above, below, left, right) + params
    return pl.pallas_call(
        front_kernel,
        grid=(strips + 1,),
        in_specs=[pl.BlockSpec(memory_space=pltpu.SMEM)]
        + [whole(a.shape) for a in args[:-2]]
        + [layer(a.shape, 0) for a in args[-2:]],
        out_specs=pl.BlockSpec(
            (1, 8, 4, 2, 16, chans), lambda i: (jnp.maximum(i - 1, 0), 0, 0, 0, 0, 0)
        ),
        out_shape=jax.ShapeDtypeStruct((strips, 8, 4, 2, 16, chans), BF),
        scratch_shapes=[
            pltpu.VMEM((2, 4 * cols_dev, 128), F32),
            pltpu.VMEM((HID // 128, rows_dev + 2, WINDOW + 2, 16, 128), F32),
            pltpu.VMEM((80, HID), F32),
            pltpu.VMEM((WINDOW * cols_dev, HID), BF),
            pltpu.VMEM((2, WINDOW * cols_dev, 128), F32),
            pltpu.VMEM((CH, CH), BF),
            pltpu.VMEM((80, HID), F32),
        ],
        compiler_params=pltpu.CompilerParams(
            dimension_semantics=("arbitrary",), vmem_limit_bytes=60 * 2**20
        ),
        name="front",
    )(edge, *args)


def grid_attention(tokens, gain, qkv, wo):
    return pl.pallas_call(
        grid_kernel,
        grid=(1,),
        in_specs=[whole(tokens.shape), whole(gain.shape), layer(qkv.shape, 1), layer(wo.shape, 1)],
        out_specs=whole(tokens.shape),
        out_shape=jax.ShapeDtypeStruct(tokens.shape, BF),
        scratch_shapes=[
            pltpu.VMEM((2, tokens.shape[0] * tokens.shape[1], 128), F32),
            pltpu.VMEM((CH, CH), BF),
        ],
        compiler_params=pltpu.CompilerParams(
            dimension_semantics=("arbitrary",), vmem_limit_bytes=40 * 2**20
        ),
        name="grid_attention",
    )(tokens, gain, qkv, wo)


def halos(image):
    rows = lax.axis_size("row")
    cols = lax.axis_size("col")
    above = lax.ppermute(image[-1], "row", [(i, i + 1) for i in range(rows - 1)])
    below = lax.ppermute(image[0], "row", [(i + 1, i) for i in range(rows - 1)])
    none = jnp.zeros((38 - image.shape[0], image.shape[2]), image.dtype)
    first = jnp.concatenate([above[:1], image[:, 0], below[:1], none], axis=0)
    last = jnp.concatenate([above[-1:], image[:, -1], below[-1:], none], axis=0)
    left = lax.ppermute(last, "col", [(i, i + 1) for i in range(cols - 1)])
    right = lax.ppermute(first, "col", [(i + 1, i) for i in range(cols - 1)])
    return above, below, left, right


def per_device(
    image,
    bn_gain,
    bn_shift,
    expand_weight,
    expand_bias,
    depth_kernel,
    depth_bias,
    project_weight,
    norm_gain,
    qkv_weight,
    out_weight,
):
    rows_dev, cols_dev, chans = image.shape
    row_at = lax.axis_index("row")
    col_at = lax.axis_index("col")
    edge = jnp.stack(
        [
            row_at > 0,
            row_at < lax.axis_size("row") - 1,
            col_at > 0,
            col_at < lax.axis_size("col") - 1,
        ]
    ).astype(jnp.int32)
    above, below, left, right = halos(image)
    params = (
        bn_gain[None],
        bn_shift[None],
        expand_weight,
        expand_bias[None],
        depth_kernel,
        depth_bias[None],
        project_weight,
        norm_gain,
        qkv_weight,
        out_weight,
    )
    after_block = front(edge, image, above, below, left, right, params)
    outgoing = after_block.reshape(128, 32, chans)
    received = lax.all_to_all(outgoing, ("row", "col"), split_axis=0, concat_axis=0, tiled=True)
    done = grid_attention(received.reshape(256, 16, chans), norm_gain, qkv_weight, out_weight)
    returned = lax.all_to_all(
        done.reshape(128, 32, chans), ("row", "col"), split_axis=0, concat_axis=0, tiled=True
    )
    placed = returned.reshape(4, 8, 4, 2, 2, 8, chans).transpose(0, 2, 4, 3, 1, 5, 6)
    return placed.reshape(rows_dev, cols_dev, chans)


def solution(mesh):
    in_specs = (P("row", "col", None), P(), P(), P(), P(), P(), P(), P(), P(), P(), P())
    out_specs = P("row", "col", None)
    return jax.shard_map(
        per_device, mesh=mesh, in_specs=in_specs, out_specs=out_specs, check_vma=False
    )
```

```python
import jax
import jax.numpy as jnp
from jax import lax
from jax.experimental import pallas as pl
from jax.experimental.pallas import tpu as pltpu
from jax.sharding import PartitionSpec as P

HEADS = 8
SETS = 4
AHEAD = 4
WAHEAD = 2


HEAD = 32
CH = 256
HID = 1024
WINDOW = 8
EPS = 1e-5
GELU_A = 0.7978845608028654
CUBE = (GELU_A * 0.044715) ** (1.0 / 3.0)
GELU_C = GELU_A / CUBE
QSCALE = 32.0**-0.5 * 1.4426950408889634
BF = jnp.bfloat16
F32 = jnp.float32


def mm(a, b, dims):
    return lax.dot_general(a, b, (dims, ((), ())), preferred_element_type=F32)


def nn(a, b):
    return mm(a, b, ((1,), (0,)))


def nt(a, b):
    return mm(a, b, ((1,), (1,)))


def tn(a, b):
    return mm(a, b, ((0,), (0,)))


def scaled_gelu(z):
    return z + z * jnp.tanh(z * (z * z + GELU_C))


def normalised(y, gain):
    mean = jnp.mean(y, axis=-1, keepdims=True)
    centred = y - mean
    spread = jnp.mean(centred * centred, axis=-1, keepdims=True)
    return centred * lax.rsqrt(spread + EPS) * gain


def run(parts):
    while parts:
        left = []
        for part, n in parts:
            for _ in range(n):
                if next(part, part) is part:
                    break
            else:
                left.append((part, n))
        parts = left


def finish(part):
    run([(part, 1)])


def turned(weight):
    return weight.astype(F32).T.astype(BF)


def store_halves(ref, at, values):
    ref[0, at, :] = values[:, :128]
    ref[1, at, :] = values[:, 128:]


def load_halves(ref, at):
    return jnp.concatenate([ref[0, at, :], ref[1, at, :]], axis=1)


def window_mix(xn, wk, weight):
    pairs = xn.shape[0] // 128
    wqv = jnp.concatenate([weight[:, :CH], weight[:, 2 * CH :]], axis=1)
    proj = nn(xn, wqv)
    query = (proj[:, :CH] * QSCALE).astype(BF)
    vals = proj[:, CH:].astype(BF)
    yield
    keys = nt(wk, xn).astype(BF)
    yield
    none = jnp.zeros((HEAD, 128), BF)
    lane = lax.broadcasted_iota(jnp.int32, (128, 128), 1)
    row = lax.broadcasted_iota(jnp.int32, (128, 128), 0)
    inside = jnp.where(lane == jnp.where(row < 64, 0, 1), 1.0, 0.0).astype(BF)
    across = (row == 0) & (lane >= 64) | (row == 1) & (lane < 64)
    across = jnp.where(across, -1e30, 0.0).astype(BF)

    def score(t, g):
        cols = []
        for j in range(4):
            h = 4 * g + j
            parts = [none] * 4
            parts[j] = keys[HEAD * h : HEAD * h + HEAD, 128 * t : 128 * t + 128]
            parts.append(across)
            cols.append(jnp.concatenate(parts, axis=0))
        left = query[128 * t : 128 * t + 128, 128 * g : 128 * g + 128]
        left = jnp.concatenate([left, inside], axis=1)
        return nn(left, jnp.concatenate(cols, axis=1))

    order = [(t, g) for t in range(pairs) for g in range(2)]
    ahead = [score(*order[n]) for n in range(WAHEAD)]
    mixed = []
    for n, (t, g) in enumerate(order):
        scores = ahead.pop(0)
        if n + WAHEAD < len(order):
            ahead.append(score(*order[n + WAHEAD]))
        v = vals[128 * t : 128 * t + 128, 128 * g : 128 * g + 128]
        probs = []
        right = []
        for j in range(4):
            part = scores[:, 128 * j : 128 * j + 128]
            top = jnp.max(part, axis=1, keepdims=True)
            probs.append(jnp.exp2(part - top).astype(BF))
            mask = (lane >= HEAD * j) & (lane < HEAD * j + HEAD)
            zero = jnp.zeros_like(v)
            right.append(
                jnp.concatenate(
                    [jnp.where(mask, v, zero), jnp.where(mask, jnp.ones_like(v), zero)], axis=1
                )
            )
        out = nn(jnp.concatenate(probs, axis=1), jnp.concatenate(right, axis=0))
        mixed.append((out[:, :128] / out[:, 128:]).astype(BF))
        yield
    return jnp.concatenate(
        [jnp.concatenate(mixed[2 * t : 2 * t + 2], axis=1) for t in range(pairs)], axis=0
    )


def grid_mix(xns, wk, weight):
    zq = jnp.zeros((HEAD, 256), BF)
    lane = lax.broadcasted_iota(jnp.int32, (256, 128), 1)
    wqv = jnp.concatenate([weight[:, :CH], weight[:, 2 * CH :]], axis=1)
    proj = [nn(xn, wqv) for xn in xns]
    keysT = [nt(wk, xn).astype(BF) for xn in xns]
    query = [(p[:, :CH] * QSCALE).astype(BF) for p in proj]
    vals = [p[:, CH:].astype(BF) for p in proj]

    def score(t, h):
        g, j = divmod(h, 4)
        parts = [zq] * 4
        parts[j] = keysT[t][HEAD * h : HEAD * h + HEAD]
        return nn(query[t][:, 128 * g : 128 * g + 128], jnp.concatenate(parts, axis=0))

    order = [(t, h) for h in range(HEADS) for t in range(len(xns))]
    ahead = [score(*order[n]) for n in range(AHEAD)]
    halves = [[] for _ in xns]
    acc = [None for _ in xns]
    for n, (t, h) in enumerate(order):
        g, j = divmod(h, 4)
        scores = ahead.pop(0)
        if n + AHEAD < len(order):
            ahead.append(score(*order[n + AHEAD]))
        top = jnp.max(scores, axis=1, keepdims=True)
        probs = jnp.exp2(scores - top).astype(BF)
        mask = (lane >= HEAD * j) & (lane < HEAD * j + HEAD)
        v = vals[t][:, 128 * g : 128 * g + 128]
        z = jnp.zeros_like(v)
        right = jnp.concatenate([jnp.where(mask, v, z), jnp.where(mask, jnp.ones_like(v), z)], axis=1)
        out = nn(probs, right)
        acc[t] = out if j == 0 else acc[t] + out
        if j == 3:
            halves[t].append((acc[t][:, :128] / acc[t][:, 128:]).astype(BF))
    return [jnp.concatenate(x, axis=1) for x in halves]


def front_kernel(
    edge_ref,
    image_ref,
    above_ref,
    below_ref,
    left_ref,
    right_ref,
    bn_gain_ref,
    bn_shift_ref,
    expand_ref,
    expand_bias_ref,
    depth_ref,
    depth_bias_ref,
    project_ref,
    gain_ref,
    qkv_ref,
    wo_ref,
    out_ref,
    line,
    hidden,
    side_hidden,
    middle,
    moved,
    wk,
    taps,
):
    step = pl.program_id(0)
    rows_dev = image_ref.shape[0]
    strips = rows_dev // WINDOW
    cell = lax.broadcasted_iota(jnp.int32, (16, 1), 0)

    def normed(values):
        return values.astype(F32) * (bn_gain_ref[...] * CUBE) + bn_shift_ref[...] * CUBE

    def activated(cells, c):
        lanes = slice(256 * c, 256 * c + 256)
        total = nn(cells, expand_ref[:, lanes]) + expand_bias_ref[:, lanes] * CUBE
        return scaled_gelu(total)

    def put(row, at, c, values):
        hidden[2 * c, row, at] = values[..., :128].astype(hidden.dtype)
        hidden[2 * c + 1, row, at] = values[..., 128:].astype(hidden.dtype)

    def expand_rows(rows, first_row, keep_at, keep):
        count = len(rows)
        for n in range(count):
            store_halves(line, slice(128 * n, 128 * n + 128), normed(rows[n]))
        cells = jnp.concatenate(
            [
                load_halves(line, pl.ds(128 * n + m, 16, stride=WINDOW))
                for n in range(count)
                for m in range(WINDOW)
            ],
            axis=0,
        ).astype(BF)
        for c in range(HID // 256):
            lanes = slice(256 * c, 256 * c + 256)
            act = activated(cells, c).reshape(count, WINDOW, 16, 256)
            yield
            for n in range(count):
                one = act[n] * keep if n == keep_at else act[n]
                row = first_row + n
                put(row, slice(1, WINDOW + 1), c, one)
                left = pltpu.roll(one[WINDOW - 1], 1, 0)
                right = pltpu.roll(one[0], 15, 0)
                left = jnp.where(cell == 0, side_hidden[pl.ds(row, 1), lanes], left)
                right = jnp.where(cell == 15, side_hidden[pl.ds(40 + row, 1), lanes], right)
                put(row, 0, c, left)
                put(row, WINDOW + 1, c, right)

    @pl.when(step == 0)
    def _():
        wk[...] = turned(qkv_ref[0, :, CH : 2 * CH])
        for tap in range(9):
            row = depth_ref[tap // 3, tap % 3 : tap % 3 + 1].astype(F32) * 0.5
            taps[8 * tap : 8 * tap + 8, :] = jnp.broadcast_to(row, (8, HID))
        taps[72:80, :] = jnp.broadcast_to(depth_bias_ref[...] * CUBE, (8, HID))
        cells = jnp.concatenate([normed(left_ref[...]), normed(right_ref[...])], axis=0).astype(BF)
        index = lax.broadcasted_iota(jnp.int32, (80, 1), 0)
        right = index >= 40
        row = jnp.where(right, index - 40, index)
        keep = jnp.where(right, edge_ref[3], edge_ref[2])
        keep = jnp.where(row == 0, keep * edge_ref[0], keep)
        keep = jnp.where(row == rows_dev + 1, keep * edge_ref[1], keep)
        keep = keep.astype(F32)
        for c in range(HID // 256):
            lanes = slice(256 * c, 256 * c + 256)
            side_hidden[:, lanes] = activated(cells, c) * keep
        finish(expand_rows([above_ref[...], image_ref[0]], 0, 0, edge_ref[0].astype(F32)))

    def expand(strip, i):
        base = strip * WINDOW + 1 + 4 * i
        rows = [image_ref[base + n] for n in range(3)]
        last = base + 3
        beyond = last == rows_dev
        final = image_ref[jnp.minimum(last, rows_dev - 1)]
        rows.append(jnp.where(beyond, below_ref[...], final))
        keep = jnp.where(beyond, edge_ref[1], 1).astype(F32)
        yield from expand_rows(rows, base + 1, 3, keep)

    def depth(strip, r):
        at = pl.ds(pl.multiple_of(r * 128, 128), 128)
        for c in range(HID // 128):
            lanes = slice(128 * c, 128 * c + 128)
            total = None
            for down in range(3):
                around = hidden[c, strip * WINDOW + r + down]
                around = around.reshape(WINDOW + 2, 2, 8, 128)
                for across in range(3):
                    tap = 8 * (3 * down + across)
                    term = around[across : across + WINDOW] * taps[tap : tap + 8, lanes]
                    total = term if total is None else total + term
            act = scaled_gelu(total + taps[72:80, lanes])
            middle[at, lanes] = act.reshape(128, 128).astype(BF)
            yield

    def project(i):
        for n in range(4):
            at = pl.ds(pl.multiple_of(512 * i + 128 * n, 128), 128)
            store_halves(moved, at, nn(middle[at, :], project_ref[...]) * (0.5 / CUBE))
            yield

    def windows(strip, i):
        pieces = []
        for p in range(4):
            col = pl.multiple_of(64 * i + 16 * p, 16)
            res = image_ref[pl.ds(strip * WINDOW, WINDOW), pl.ds(col, 16), :].astype(F32)
            res = res.reshape(WINDOW, 2, WINDOW, CH)
            for w in range(2):
                conv = load_halves(moved, pl.ds(2 * (4 * i + p) + w, 64, stride=16))
                pieces.append(res[:, w].reshape(64, CH) + conv)
        y = jnp.concatenate(pieces, axis=0)
        xn = normalised(y, gain_ref[0:1]).astype(BF)
        yield
        mixed = yield from window_mix(xn, wk[...], qkv_ref[0])
        y = (y + nn(mixed, wo_ref[0])).astype(BF)
        out_ref[0, :, :, i] = y.reshape(8, 4, 16, CH)

    def halves(*parts):
        def body(i, carry):
            run([(part(i), n) for part, n in parts])
            return carry

        lax.fori_loop(0, 2, body, 0)

    def depth_half(i):
        for n in range(4):
            yield from depth(step, 4 * i + n)

    def windows_half(i):
        return windows(step - 1, i)

    def expand_half(i):
        return expand(step + 1, i)

    @pl.when(step == 0)
    def _():
        halves((lambda i: expand(0, i), 1))
        halves((depth_half, 1))

    @pl.when((step > 0) & (step < strips))
    def _():
        halves((windows_half, 1), (depth_half, 3))

    @pl.when(step == strips)
    def _():
        halves((windows_half, 1))

    @pl.when(step < strips - 1)
    def _():
        halves((project, 1), (expand_half, 1))

    @pl.when(step == strips - 1)
    def _():
        halves((project, 1))


def grid_kernel(tokens_ref, gain_ref, qkv_ref, wo_ref, out_ref, work, wk):
    wk[...] = turned(qkv_ref[0, :, CH : 2 * CH])

    def spread_step(i, carry):
        at = pl.ds(pl.multiple_of(16 * i, 16), 16)
        y = tokens_ref[at].astype(F32).reshape(256, CH)
        store_halves(work, pl.ds(pl.multiple_of(256 * i, 256), 256), y)
        return carry

    lax.fori_loop(0, 16, spread_step, 0)

    def set_step(k, carry):
        ats = [pl.ds(SETS * k + n, 256, stride=16) for n in range(SETS)]
        xns = [normalised(load_halves(work, at), gain_ref[1:2]).astype(BF) for at in ats]
        mixed = grid_mix(xns, wk[...], qkv_ref[0])
        for n in range(SETS):
            store_halves(work, ats[n], load_halves(work, ats[n]) + nn(mixed[n], wo_ref[0]))
        return carry

    lax.fori_loop(0, 16 // SETS, set_step, 0)

    def collect_step(i, carry):
        at = pl.ds(pl.multiple_of(16 * i, 16), 16)
        y = load_halves(work, pl.ds(pl.multiple_of(256 * i, 256), 256))
        out_ref[at] = y.reshape(16, 16, CH).astype(BF)
        return carry

    lax.fori_loop(0, 16, collect_step, 0)


def whole(shape):
    return pl.BlockSpec(shape, lambda i: (0,) * len(shape))


def layer(shape, n):
    return pl.BlockSpec((1,) + shape[1:], lambda i: (n,) + (0,) * (len(shape) - 1))


def front(edge, image, above, below, left, right, params):
    rows_dev, cols_dev, chans = image.shape
    strips = rows_dev // WINDOW
    args = (image, above, below, left, right) + params
    return pl.pallas_call(
        front_kernel,
        grid=(strips + 1,),
        in_specs=[pl.BlockSpec(memory_space=pltpu.SMEM)]
        + [whole(a.shape) for a in args[:-2]]
        + [layer(a.shape, 0) for a in args[-2:]],
        out_specs=pl.BlockSpec(
            (1, 8, 4, 2, 16, chans), lambda i: (jnp.maximum(i - 1, 0), 0, 0, 0, 0, 0)
        ),
        out_shape=jax.ShapeDtypeStruct((strips, 8, 4, 2, 16, chans), BF),
        scratch_shapes=[
            pltpu.VMEM((2, 4 * cols_dev, 128), F32),
            pltpu.VMEM((HID // 128, rows_dev + 2, WINDOW + 2, 16, 128), F32),
            pltpu.VMEM((80, HID), F32),
            pltpu.VMEM((WINDOW * cols_dev, HID), BF),
            pltpu.VMEM((2, WINDOW * cols_dev, 128), F32),
            pltpu.VMEM((CH, CH), BF),
            pltpu.VMEM((80, HID), F32),
        ],
        compiler_params=pltpu.CompilerParams(
            dimension_semantics=("arbitrary",), vmem_limit_bytes=60 * 2**20
        ),
        name="front",
    )(edge, *args)


def grid_attention(tokens, gain, qkv, wo):
    return pl.pallas_call(
        grid_kernel,
        grid=(1,),
        in_specs=[whole(tokens.shape), whole(gain.shape), layer(qkv.shape, 1), layer(wo.shape, 1)],
        out_specs=whole(tokens.shape),
        out_shape=jax.ShapeDtypeStruct(tokens.shape, BF),
        scratch_shapes=[
            pltpu.VMEM((2, tokens.shape[0] * tokens.shape[1], 128), F32),
            pltpu.VMEM((CH, CH), BF),
        ],
        compiler_params=pltpu.CompilerParams(
            dimension_semantics=("arbitrary",), vmem_limit_bytes=40 * 2**20
        ),
        name="grid_attention",
    )(tokens, gain, qkv, wo)


def halos(image):
    rows = lax.axis_size("row")
    cols = lax.axis_size("col")
    above = lax.ppermute(image[-1], "row", [(i, (i + 1) % rows) for i in range(rows)])
    below = lax.ppermute(image[0], "row", [((i + 1) % rows, i) for i in range(rows)])
    none = jnp.zeros((38 - image.shape[0], image.shape[2]), image.dtype)
    first = jnp.concatenate([above[:1], image[:, 0], below[:1], none], axis=0)
    last = jnp.concatenate([above[-1:], image[:, -1], below[-1:], none], axis=0)
    left = lax.ppermute(last, "col", [(i, (i + 1) % cols) for i in range(cols)])
    right = lax.ppermute(first, "col", [((i + 1) % cols, i) for i in range(cols)])
    return above, below, left, right


def per_device(
    image,
    bn_gain,
    bn_shift,
    expand_weight,
    expand_bias,
    depth_kernel,
    depth_bias,
    project_weight,
    norm_gain,
    qkv_weight,
    out_weight,
):
    rows_dev, cols_dev, chans = image.shape
    row_at = lax.axis_index("row")
    col_at = lax.axis_index("col")
    edge = jnp.stack(
        [
            row_at > 0,
            row_at < lax.axis_size("row") - 1,
            col_at > 0,
            col_at < lax.axis_size("col") - 1,
        ]
    ).astype(jnp.int32)
    above, below, left, right = halos(image)
    params = (
        bn_gain[None],
        bn_shift[None],
        expand_weight,
        expand_bias[None],
        depth_kernel,
        depth_bias[None],
        project_weight,
        norm_gain,
        qkv_weight,
        out_weight,
    )
    after_block = front(edge, image, above, below, left, right, params)
    outgoing = after_block.reshape(128, 32, chans)
    received = lax.all_to_all(outgoing, ("row", "col"), split_axis=0, concat_axis=0, tiled=True)
    done = grid_attention(received.reshape(256, 16, chans), norm_gain, qkv_weight, out_weight)
    returned = lax.all_to_all(
        done.reshape(128, 32, chans), ("row", "col"), split_axis=0, concat_axis=0, tiled=True
    )
    placed = returned.reshape(4, 8, 4, 2, 2, 8, chans).transpose(0, 2, 4, 3, 1, 5, 6)
    return placed.reshape(rows_dev, cols_dev, chans)


def solution(mesh):
    in_specs = (P("row", "col", None), P(), P(), P(), P(), P(), P(), P(), P(), P(), P())
    out_specs = P("row", "col", None)
    return jax.shard_map(
        per_device, mesh=mesh, in_specs=in_specs, out_specs=out_specs, check_vma=False
    )
```

```python
import jax
import jax.numpy as jnp
from jax import lax
from jax.experimental import pallas as pl
from jax.experimental.pallas import tpu as pltpu
from jax.sharding import PartitionSpec as P

HEADS = 8
SETS = 4
AHEAD = 4
WAHEAD = 2


HEAD = 32
CH = 256
HID = 1024
WINDOW = 8
EPS = 1e-5
GELU_A = 0.7978845608028654
CUBE = (GELU_A * 0.044715) ** (1.0 / 3.0)
GELU_C = GELU_A / CUBE
QSCALE = 32.0**-0.5 * 1.4426950408889634
BF = jnp.bfloat16
F32 = jnp.float32


def mm(a, b, dims):
    return lax.dot_general(a, b, (dims, ((), ())), preferred_element_type=F32)


def nn(a, b):
    return mm(a, b, ((1,), (0,)))


def nt(a, b):
    return mm(a, b, ((1,), (1,)))


def tn(a, b):
    return mm(a, b, ((0,), (0,)))


def scaled_gelu(z):
    return z + z * jnp.tanh(z * (z * z + GELU_C))


def normalised(y, gain):
    mean = jnp.mean(y, axis=-1, keepdims=True)
    centred = y - mean
    spread = jnp.mean(centred * centred, axis=-1, keepdims=True)
    return centred * lax.rsqrt(spread + EPS) * gain


def run(parts):
    while parts:
        left = []
        for part, n in parts:
            for _ in range(n):
                if next(part, part) is part:
                    break
            else:
                left.append((part, n))
        parts = left


def finish(part):
    run([(part, 1)])


def turned(weight):
    return weight.astype(F32).T.astype(BF)


def store_halves(ref, at, values):
    ref[0, at, :] = values[:, :128]
    ref[1, at, :] = values[:, 128:]


def load_halves(ref, at):
    return jnp.concatenate([ref[0, at, :], ref[1, at, :]], axis=1)


def window_mix(xn, wk, weight):
    pairs = xn.shape[0] // 128
    wqv = jnp.concatenate([weight[:, :CH], weight[:, 2 * CH :]], axis=1)
    proj = nn(xn, wqv)
    query = (proj[:, :CH] * QSCALE).astype(BF)
    vals = proj[:, CH:].astype(BF)
    yield
    keys = nt(wk, xn).astype(BF)
    yield
    none = jnp.zeros((HEAD, 128), BF)
    lane = lax.broadcasted_iota(jnp.int32, (128, 128), 1)
    row = lax.broadcasted_iota(jnp.int32, (128, 128), 0)
    inside = jnp.where(lane == jnp.where(row < 64, 0, 1), 1.0, 0.0).astype(BF)
    across = (row == 0) & (lane >= 64) | (row == 1) & (lane < 64)
    across = jnp.where(across, -1e30, 0.0).astype(BF)

    def score(t, g):
        cols = []
        for j in range(4):
            h = 4 * g + j
            parts = [none] * 4
            parts[j] = keys[HEAD * h : HEAD * h + HEAD, 128 * t : 128 * t + 128]
            parts.append(across)
            cols.append(jnp.concatenate(parts, axis=0))
        left = query[128 * t : 128 * t + 128, 128 * g : 128 * g + 128]
        left = jnp.concatenate([left, inside], axis=1)
        return nn(left, jnp.concatenate(cols, axis=1))

    order = [(t, g) for t in range(pairs) for g in range(2)]
    ahead = [score(*order[n]) for n in range(WAHEAD)]
    mixed = []
    for n, (t, g) in enumerate(order):
        scores = ahead.pop(0)
        if n + WAHEAD < len(order):
            ahead.append(score(*order[n + WAHEAD]))
        v = vals[128 * t : 128 * t + 128, 128 * g : 128 * g + 128]
        probs = []
        right = []
        for j in range(4):
            part = scores[:, 128 * j : 128 * j + 128]
            top = jnp.max(part, axis=1, keepdims=True)
            probs.append(jnp.exp2(part - top).astype(BF))
            mask = (lane >= HEAD * j) & (lane < HEAD * j + HEAD)
            zero = jnp.zeros_like(v)
            right.append(
                jnp.concatenate(
                    [jnp.where(mask, v, zero), jnp.where(mask, jnp.ones_like(v), zero)], axis=1
                )
            )
        out = nn(jnp.concatenate(probs, axis=1), jnp.concatenate(right, axis=0))
        mixed.append((out[:, :128] / out[:, 128:]).astype(BF))
        yield
    return jnp.concatenate(
        [jnp.concatenate(mixed[2 * t : 2 * t + 2], axis=1) for t in range(pairs)], axis=0
    )


def grid_mix(xns, wk, weight):
    zq = jnp.zeros((HEAD, 256), BF)
    lane = lax.broadcasted_iota(jnp.int32, (256, 128), 1)
    wqv = jnp.concatenate([weight[:, :CH], weight[:, 2 * CH :]], axis=1)
    proj = [nn(xn, wqv) for xn in xns]
    keysT = [nt(wk, xn).astype(BF) for xn in xns]
    query = [(p[:, :CH] * QSCALE).astype(BF) for p in proj]
    vals = [p[:, CH:].astype(BF) for p in proj]

    def score(t, h):
        g, j = divmod(h, 4)
        parts = [zq] * 4
        parts[j] = keysT[t][HEAD * h : HEAD * h + HEAD]
        return nn(query[t][:, 128 * g : 128 * g + 128], jnp.concatenate(parts, axis=0))

    order = [(t, h) for h in range(HEADS) for t in range(len(xns))]
    ahead = [score(*order[n]) for n in range(AHEAD)]
    halves = [[] for _ in xns]
    acc = [None for _ in xns]
    for n, (t, h) in enumerate(order):
        g, j = divmod(h, 4)
        scores = ahead.pop(0)
        if n + AHEAD < len(order):
            ahead.append(score(*order[n + AHEAD]))
        top = jnp.max(scores, axis=1, keepdims=True)
        probs = jnp.exp2(scores - top).astype(BF)
        mask = (lane >= HEAD * j) & (lane < HEAD * j + HEAD)
        v = vals[t][:, 128 * g : 128 * g + 128]
        z = jnp.zeros_like(v)
        right = jnp.concatenate([jnp.where(mask, v, z), jnp.where(mask, jnp.ones_like(v), z)], axis=1)
        out = nn(probs, right)
        acc[t] = out if j == 0 else acc[t] + out
        if j == 3:
            halves[t].append((acc[t][:, :128] / acc[t][:, 128:]).astype(BF))
    return [jnp.concatenate(x, axis=1) for x in halves]


def front_kernel(
    image_ref,
    above_ref,
    below_ref,
    left_ref,
    right_ref,
    bn_gain_ref,
    bn_shift_ref,
    expand_ref,
    expand_bias_ref,
    depth_ref,
    depth_bias_ref,
    project_ref,
    gain_ref,
    qkv_ref,
    wo_ref,
    out_ref,
    line,
    hidden,
    side_hidden,
    middle,
    moved,
    wk,
    taps,
):
    step = pl.program_id(0)
    row_at = lax.axis_index("row")
    col_at = lax.axis_index("col")
    edge_ref = [
        jnp.where(row_at > 0, 1, 0),
        jnp.where(row_at < lax.axis_size("row") - 1, 1, 0),
        jnp.where(col_at > 0, 1, 0),
        jnp.where(col_at < lax.axis_size("col") - 1, 1, 0),
    ]
    rows_dev = image_ref.shape[0]
    strips = rows_dev // WINDOW
    cell = lax.broadcasted_iota(jnp.int32, (16, 1), 0)

    def normed(values):
        return values.astype(F32) * (bn_gain_ref[...] * CUBE) + bn_shift_ref[...] * CUBE

    def activated(cells, c):
        lanes = slice(256 * c, 256 * c + 256)
        total = nn(cells, expand_ref[:, lanes]) + expand_bias_ref[:, lanes] * CUBE
        return scaled_gelu(total)

    def put(row, at, c, values):
        hidden[2 * c, row, at] = values[..., :128].astype(hidden.dtype)
        hidden[2 * c + 1, row, at] = values[..., 128:].astype(hidden.dtype)

    def expand_rows(rows, first_row, keep_at, keep):
        count = len(rows)
        for n in range(count):
            store_halves(line, slice(128 * n, 128 * n + 128), normed(rows[n]))
        cells = jnp.concatenate(
            [
                load_halves(line, pl.ds(128 * n + m, 16, stride=WINDOW))
                for n in range(count)
                for m in range(WINDOW)
            ],
            axis=0,
        ).astype(BF)
        for c in range(HID // 256):
            lanes = slice(256 * c, 256 * c + 256)
            act = activated(cells, c).reshape(count, WINDOW, 16, 256)
            yield
            for n in range(count):
                one = act[n] * keep if n == keep_at else act[n]
                row = first_row + n
                put(row, slice(1, WINDOW + 1), c, one)
                left = pltpu.roll(one[WINDOW - 1], 1, 0)
                right = pltpu.roll(one[0], 15, 0)
                left = jnp.where(cell == 0, side_hidden[pl.ds(row, 1), lanes], left)
                right = jnp.where(cell == 15, side_hidden[pl.ds(40 + row, 1), lanes], right)
                put(row, 0, c, left)
                put(row, WINDOW + 1, c, right)

    @pl.when(step == 0)
    def _():
        wk[...] = turned(qkv_ref[0, :, CH : 2 * CH])
        for tap in range(9):
            row = depth_ref[tap // 3, tap % 3 : tap % 3 + 1].astype(F32) * 0.5
            taps[8 * tap : 8 * tap + 8, :] = jnp.broadcast_to(row, (8, HID))
        taps[72:80, :] = jnp.broadcast_to(depth_bias_ref[...] * CUBE, (8, HID))
        cells = jnp.concatenate([normed(left_ref[...]), normed(right_ref[...])], axis=0).astype(BF)
        index = lax.broadcasted_iota(jnp.int32, (80, 1), 0)
        right = index >= 40
        row = jnp.where(right, index - 40, index)
        keep = jnp.where(right, edge_ref[3], edge_ref[2])
        keep = jnp.where(row == 0, keep * edge_ref[0], keep)
        keep = jnp.where(row == rows_dev + 1, keep * edge_ref[1], keep)
        keep = keep.astype(F32)
        for c in range(HID // 256):
            lanes = slice(256 * c, 256 * c + 256)
            side_hidden[:, lanes] = activated(cells, c) * keep
        finish(expand_rows([above_ref[...], image_ref[0]], 0, 0, edge_ref[0].astype(F32)))

    def expand(strip, i):
        base = strip * WINDOW + 1 + 4 * i
        rows = [image_ref[base + n] for n in range(3)]
        last = base + 3
        beyond = last == rows_dev
        final = image_ref[jnp.minimum(last, rows_dev - 1)]
        rows.append(jnp.where(beyond, below_ref[...], final))
        keep = jnp.where(beyond, edge_ref[1], 1).astype(F32)
        yield from expand_rows(rows, base + 1, 3, keep)

    def depth(strip, r):
        at = pl.ds(pl.multiple_of(r * 128, 128), 128)
        for c in range(HID // 128):
            lanes = slice(128 * c, 128 * c + 128)
            total = None
            for down in range(3):
                around = hidden[c, strip * WINDOW + r + down]
                around = around.reshape(WINDOW + 2, 2, 8, 128)
                for across in range(3):
                    tap = 8 * (3 * down + across)
                    term = around[across : across + WINDOW] * taps[tap : tap + 8, lanes]
                    total = term if total is None else total + term
            act = scaled_gelu(total + taps[72:80, lanes])
            middle[at, lanes] = act.reshape(128, 128).astype(BF)
            yield

    def project(i):
        for n in range(4):
            at = pl.ds(pl.multiple_of(512 * i + 128 * n, 128), 128)
            store_halves(moved, at, nn(middle[at, :], project_ref[...]) * (0.5 / CUBE))
            yield

    def windows(strip, i):
        pieces = []
        for p in range(4):
            col = pl.multiple_of(64 * i + 16 * p, 16)
            res = image_ref[pl.ds(strip * WINDOW, WINDOW), pl.ds(col, 16), :].astype(F32)
            res = res.reshape(WINDOW, 2, WINDOW, CH)
            for w in range(2):
                conv = load_halves(moved, pl.ds(2 * (4 * i + p) + w, 64, stride=16))
                pieces.append(res[:, w].reshape(64, CH) + conv)
        y = jnp.concatenate(pieces, axis=0)
        xn = normalised(y, gain_ref[0:1]).astype(BF)
        yield
        mixed = yield from window_mix(xn, wk[...], qkv_ref[0])
        y = (y + nn(mixed, wo_ref[0])).astype(BF)
        out_ref[0, :, :, i] = y.reshape(8, 4, 16, CH)

    def halves(*parts):
        def body(i, carry):
            run([(part(i), n) for part, n in parts])
            return carry

        lax.fori_loop(0, 2, body, 0)

    def depth_half(i):
        for n in range(4):
            yield from depth(step, 4 * i + n)

    def windows_half(i):
        return windows(step - 1, i)

    def expand_half(i):
        return expand(step + 1, i)

    @pl.when(step == 0)
    def _():
        halves((lambda i: expand(0, i), 1))
        halves((depth_half, 1))

    @pl.when((step > 0) & (step < strips))
    def _():
        halves((windows_half, 1), (depth_half, 3))

    @pl.when(step == strips)
    def _():
        halves((windows_half, 1))

    @pl.when(step < strips - 1)
    def _():
        halves((project, 1), (expand_half, 1))

    @pl.when(step == strips - 1)
    def _():
        halves((project, 1))


def grid_kernel(tokens_ref, gain_ref, qkv_ref, wo_ref, out_ref, work, wk):
    wk[...] = turned(qkv_ref[0, :, CH : 2 * CH])

    def spread_step(i, carry):
        at = pl.ds(pl.multiple_of(16 * i, 16), 16)
        y = tokens_ref[at].astype(F32).reshape(256, CH)
        store_halves(work, pl.ds(pl.multiple_of(256 * i, 256), 256), y)
        return carry

    lax.fori_loop(0, 16, spread_step, 0)

    def set_step(k, carry):
        ats = [pl.ds(SETS * k + n, 256, stride=16) for n in range(SETS)]
        xns = [normalised(load_halves(work, at), gain_ref[1:2]).astype(BF) for at in ats]
        mixed = grid_mix(xns, wk[...], qkv_ref[0])
        for n in range(SETS):
            store_halves(work, ats[n], load_halves(work, ats[n]) + nn(mixed[n], wo_ref[0]))
        return carry

    lax.fori_loop(0, 16 // SETS, set_step, 0)

    def collect_step(i, carry):
        at = pl.ds(pl.multiple_of(16 * i, 16), 16)
        y = load_halves(work, pl.ds(pl.multiple_of(256 * i, 256), 256))
        out_ref[at] = y.reshape(16, 16, CH).astype(BF)
        return carry

    lax.fori_loop(0, 16, collect_step, 0)


def whole(shape):
    return pl.BlockSpec(shape, lambda i: (0,) * len(shape))


def layer(shape, n):
    return pl.BlockSpec((1,) + shape[1:], lambda i: (n,) + (0,) * (len(shape) - 1))


def front(image, above, below, left, right, params):
    rows_dev, cols_dev, chans = image.shape
    strips = rows_dev // WINDOW
    args = (image, above, below, left, right) + params
    return pl.pallas_call(
        front_kernel,
        grid=(strips + 1,),
        in_specs=[whole(a.shape) for a in args[:-2]]
        + [layer(a.shape, 0) for a in args[-2:]],
        out_specs=pl.BlockSpec(
            (1, 8, 4, 2, 16, chans), lambda i: (jnp.maximum(i - 1, 0), 0, 0, 0, 0, 0)
        ),
        out_shape=jax.ShapeDtypeStruct((strips, 8, 4, 2, 16, chans), BF),
        scratch_shapes=[
            pltpu.VMEM((2, 4 * cols_dev, 128), F32),
            pltpu.VMEM((HID // 128, rows_dev + 2, WINDOW + 2, 16, 128), F32),
            pltpu.VMEM((80, HID), F32),
            pltpu.VMEM((WINDOW * cols_dev, HID), BF),
            pltpu.VMEM((2, WINDOW * cols_dev, 128), F32),
            pltpu.VMEM((CH, CH), BF),
            pltpu.VMEM((80, HID), F32),
        ],
        compiler_params=pltpu.CompilerParams(
            dimension_semantics=("arbitrary",), vmem_limit_bytes=60 * 2**20
        ),
        name="front",
    )(*args)


def grid_attention(tokens, gain, qkv, wo):
    return pl.pallas_call(
        grid_kernel,
        grid=(1,),
        in_specs=[whole(tokens.shape), whole(gain.shape), layer(qkv.shape, 1), layer(wo.shape, 1)],
        out_specs=whole(tokens.shape),
        out_shape=jax.ShapeDtypeStruct(tokens.shape, BF),
        scratch_shapes=[
            pltpu.VMEM((2, tokens.shape[0] * tokens.shape[1], 128), F32),
            pltpu.VMEM((CH, CH), BF),
        ],
        compiler_params=pltpu.CompilerParams(
            dimension_semantics=("arbitrary",), vmem_limit_bytes=40 * 2**20
        ),
        name="grid_attention",
    )(tokens, gain, qkv, wo)


def halos(image):
    rows = lax.axis_size("row")
    cols = lax.axis_size("col")
    above = lax.ppermute(image[-1], "row", [(i, (i + 1) % rows) for i in range(rows)])
    below = lax.ppermute(image[0], "row", [((i + 1) % rows, i) for i in range(rows)])
    none = jnp.zeros((38 - image.shape[0], image.shape[2]), image.dtype)
    first = jnp.concatenate([above[:1], image[:, 0], below[:1], none], axis=0)
    last = jnp.concatenate([above[-1:], image[:, -1], below[-1:], none], axis=0)
    left = lax.ppermute(last, "col", [(i, (i + 1) % cols) for i in range(cols)])
    right = lax.ppermute(first, "col", [((i + 1) % cols, i) for i in range(cols)])
    return above, below, left, right


def per_device(
    image,
    bn_gain,
    bn_shift,
    expand_weight,
    expand_bias,
    depth_kernel,
    depth_bias,
    project_weight,
    norm_gain,
    qkv_weight,
    out_weight,
):
    rows_dev, cols_dev, chans = image.shape
    above, below, left, right = halos(image)
    params = (
        bn_gain[None],
        bn_shift[None],
        expand_weight,
        expand_bias[None],
        depth_kernel,
        depth_bias[None],
        project_weight,
        norm_gain,
        qkv_weight,
        out_weight,
    )
    after_block = front(image, above, below, left, right, params)
    outgoing = after_block.reshape(128, 32, chans)
    received = lax.all_to_all(outgoing, ("row", "col"), split_axis=0, concat_axis=0, tiled=True)
    done = grid_attention(received.reshape(256, 16, chans), norm_gain, qkv_weight, out_weight)
    returned = lax.all_to_all(
        done.reshape(128, 32, chans), ("row", "col"), split_axis=0, concat_axis=0, tiled=True
    )
    placed = returned.reshape(4, 8, 4, 2, 2, 8, chans).transpose(0, 2, 4, 3, 1, 5, 6)
    return placed.reshape(rows_dev, cols_dev, chans)


def solution(mesh):
    in_specs = (P("row", "col", None), P(), P(), P(), P(), P(), P(), P(), P(), P(), P())
    out_specs = P("row", "col", None)
    return jax.shard_map(
        per_device, mesh=mesh, in_specs=in_specs, out_specs=out_specs, check_vma=False
    )
```
